256 devices in a mesh: gx: 8 (over x, core), gy: 32 (over z, y).
Axes of the slice: x: 4, y: 4, z: 8, core: 2. Of those that a mesh axis runs over, the one named last changes fastest.
Arguments:
- volume: bfloat16 [64, 64, 64, 128], P('gx', 'gy'), may hold values from -6 to 6
- weight_entry: bfloat16 [3, 3, 3, 128, 128], replicated, may hold values from -0.15625 to 0.15625
- weight_down: bfloat16 [2, 2, 2, 128, 256], replicated, may hold values from -0.25 to 0.25
- weight_deep_first: bfloat16 [3, 3, 3, 256, 256], replicated, may hold values from -0.109375 to 0.109375
- weight_deep_second: bfloat16 [3, 3, 3, 256, 256], replicated, may hold values from -0.109375 to 0.109375
- weight_upward: bfloat16 [2, 2, 2, 256, 128], replicated, may hold values from -0.5 to 0.5
- weight_decoder: bfloat16 [3, 3, 3, 256, 128], replicated, may hold values from -0.109375 to 0.109375
Outputs:
- decoded: bfloat16 [64, 64, 64, 128], P('gx', 'gy')
The draws below stay inside these ranges and needn't reach their ends.
All inputs are finite; a program needn't handle non-finite values.
Results may differ from the reference program's by a relative error of at most 0.013.
Values may be sent and summed in bfloat16 or wider, within the bound.
No kernel may reach another device: no remote copies, remote signals or barrier semaphores. Data moves between devices by JAX's collectives and lax.ppermute only.
A program may use at most 64 MiB of HBM per device.

```python
import jax
import jax.numpy as jnp
from jax import lax

C4 = 128
C5 = 256
DEPTH = 64
NX = 64
NY = 64


def shard_levels(stream_key, shape, shards, least, high):
    loudness = 1.0
    for position, shards_of in shards:
        steps = jax.random.uniform(jax.random.fold_in(jax.random.fold_in(stream_key, 6), position), (shards_of,), jnp.float32, least / len(shards), high / len(shards))
        loudness = loudness * jnp.repeat(jnp.exp(steps), shape[position] // shards_of).reshape((-1,) + (1,) * (len(shape) - 1 - position))
    return loudness


def normal_values(stream_key, dims, spread, reach, split=(), kind=jnp.bfloat16):
    array = jax.random.normal(stream_key, dims, jnp.float32) * spread
    if len(split) > 0:
        array = shard_levels(stream_key, dims, split, -0.22, 0.18) * array
    return jnp.clip(array, min=-reach, max=reach).astype(kind)


def setup_inputs(seed: int = 0) -> dict:
    splits = jax.random.split(jax.random.key(seed), 8)
    return {
        "volume": normal_values(splits[0], (NX, NY, DEPTH, C4), 1.0, 6.0, ((0, 8), (1, 32))),
        "weight_entry": normal_values(splits[1], (3, 3, 3, C4, C4), (27 * C4 // 2) ** -0.5, 0.15625),
        "weight_down": normal_values(splits[2], (2, 2, 2, C4, C5), (4 * C4) ** -0.5, 0.25),
        "weight_deep_first": normal_values(splits[3], (3, 3, 3, C5, C5), (27 * C5 // 2) ** -0.5, 0.109375),
        "weight_deep_second": normal_values(splits[4], (3, 3, 3, C5, C5), (27 * C5 // 2) ** -0.5, 0.109375),
        "weight_upward": normal_values(splits[5], (2, 2, 2, C5, C4), (C5 // 2) ** -0.5, 0.5),
        "weight_decoder": normal_values(splits[6], (3, 3, 3, 2 * C4, C4), (27 * C4) ** -0.5, 0.109375),
    }


def leaky_unit(values):
    return jnp.where(values > 0, values, 0.1 * values)


def conv_cube(inputs, weight):
    result = lax.conv_general_dilated(inputs.astype(jnp.float32)[None], weight.astype(jnp.float32), (1, 1, 1), "SAME", dimension_numbers=("NDHWC", "DHWIO", "NDHWC"), precision=lax.Precision.HIGHEST)
    return result[0]


def down_sample(inputs, weight):
    blocks = inputs.astype(jnp.float32).reshape(inputs.shape[0] // 2, 2, inputs.shape[1] // 2, 2, inputs.shape[2] // 2, 2, inputs.shape[3])
    return jnp.einsum("iajbkdc,abdco->ijko", blocks, weight.astype(jnp.float32), precision=lax.Precision.HIGHEST)


def up_sample(inputs, weight):
    result = jnp.einsum("ijkc,abdco->iajbkdo", inputs.astype(jnp.float32), weight.astype(jnp.float32), precision=lax.Precision.HIGHEST)
    return result.reshape(2 * inputs.shape[0], 2 * inputs.shape[1], 2 * inputs.shape[2], weight.shape[4])


def reference(volume, weight_entry, weight_down, weight_deep_first, weight_deep_second, weight_upward, weight_decoder):
    encoded = leaky_unit(conv_cube(volume, weight_entry)).astype(jnp.bfloat16)
    coarse = leaky_unit(down_sample(encoded, weight_down)).astype(jnp.bfloat16)
    deep_one = leaky_unit(conv_cube(coarse, weight_deep_first)).astype(jnp.bfloat16)
    deep_two = leaky_unit(conv_cube(deep_one, weight_deep_second)).astype(jnp.bfloat16)
    upward = leaky_unit(up_sample(deep_two, weight_upward)).astype(jnp.bfloat16)
    joined = jnp.concatenate([upward, encoded], axis=3)
    return leaky_unit(conv_cube(joined, weight_decoder)).astype(jnp.bfloat16)
```

```python
import jax
import jax.numpy as jnp
from jax import lax
from jax.experimental import pallas as pl
from jax.experimental.pallas import tpu as pltpu
from jax.sharding import PartitionSpec as P

BF = jnp.bfloat16
F32 = jnp.float32
LIMIT = 48 * 1024 * 1024


def leaky_unit(values):
    return jnp.where(values > 0, values, 0.1 * values)


def inside(index, count):
    return (index >= 0) & (index < count)


def depth_taps(cells):
    depth = cells.shape[0]
    at = lax.broadcasted_iota(jnp.int32, cells.shape, 0)
    before = jnp.where(at == 0, 0.0, pltpu.roll(cells, 1, axis=0))
    after = jnp.where(at == depth - 1, 0.0, pltpu.roll(cells, depth - 1, axis=0))
    return before.astype(BF), cells.astype(BF), after.astype(BF)


def entry_kernel(own, y1, y2, x1, x2, weight, down, encoded, coarse, stacked, fine):
    gx, gy = lax.axis_index("gx"), lax.axis_index("gy")
    odd_x, odd_y = lax.rem(gx, 2) == 1, lax.rem(gy, 2) == 1
    nx, ny = lax.axis_size("gx"), lax.axis_size("gy")

    def put(row, col, cells):
        for tap, part in enumerate(depth_taps(cells)):
            lane = (col * 3 + tap) * 128
            stacked[row, :, lane : lane + 128] = part

    def one_row(i, carry):
        first, second = y1[i].astype(F32), y2[i].astype(F32)
        low = jnp.where(odd_y, first, second)
        high = jnp.where(odd_y, second, first)
        put(i + 1, 0, jnp.where(gy > 0, low, 0.0))
        put(i + 1, 1, own[i, 0].astype(F32))
        put(i + 1, 2, own[i, 1].astype(F32))
        put(i + 1, 3, jnp.where(gy < ny - 1, high, 0.0))
        return carry

    lax.fori_loop(0, 8, one_row, 0)
    for col in range(4):
        first, second = x1[col].astype(F32), x2[col].astype(F32)
        low = jnp.where(odd_x, first, second)
        high = jnp.where(odd_x, second, first)
        ok = inside(gy * 2 - 1 + col, ny * 2)
        put(0, col, jnp.where(ok & (gx > 0), low, 0.0))
        put(9, col, jnp.where(ok & (gx < nx - 1), high, 0.0))

    total = jnp.zeros((512, 256), F32)
    for off in range(3):
        total = total + jnp.dot(
            stacked[off : off + 8].reshape(512, 1536), weight[off], preferred_element_type=F32
        )
    result = leaky_unit(total).astype(BF).reshape(8, 64, 256)
    for b in range(2):
        half = result[:, :, b * 128 : b * 128 + 128]
        encoded[:, b] = half
        fine[:, b] = half.astype(F32)
    small = jnp.zeros((128, 256), F32)
    for a in range(2):
        for d in range(2):
            cells = jnp.concatenate(
                [
                    jnp.concatenate(
                        [fine[2 * i + a, b, pl.ds(d, 32, stride=2), :] for b in range(2)], axis=1
                    )
                    for i in range(4)
                ],
                axis=0,
            ).astype(BF)
            small = small + jnp.dot(
                cells, down[a, :, d].reshape(256, 256), preferred_element_type=F32
            )
    coarse[...] = leaky_unit(small).astype(BF).reshape(4, 32, 256)


def fill_deep(rows, first_row, planes, stacked):
    gy = lax.axis_index("gy")
    nx, ny = lax.axis_size("gx"), lax.axis_size("gy")

    for row in range(rows):
        ok_row = inside(first_row + row, nx * 4)
        for plane, cells in enumerate(planes(row)):
            ok = ok_row & inside(gy - 1 + plane, ny)
            for tap, part in enumerate(depth_taps(jnp.where(ok, cells, 0.0))):
                lane = (plane * 3 + tap) * 256
                stacked[row, :, lane : lane + 256] = part


def deep_conv(rows, stacked, weight, out):
    total = jnp.zeros((rows * 32, 256), F32)
    for off in range(3):
        total = total + jnp.dot(
            stacked[off : off + rows].reshape(rows * 32, 2304),
            weight[off],
            preferred_element_type=F32,
        )
    out[...] = leaky_unit(total).astype(BF).reshape(rows, 32, 256)


def first_kernel(own, y1, y2, x1, x2, weight, out, stacked):
    gx, gy = lax.axis_index("gx"), lax.axis_index("gy")
    odd_x, odd_y = lax.rem(gx, 2) == 1, lax.rem(gy, 2) == 1

    def planes(row):
        if 3 <= row < 7:
            first, second = y1[row - 3].astype(F32), y2[row - 3].astype(F32)
            return (
                jnp.where(odd_y, first, second),
                own[row - 3].astype(F32),
                jnp.where(odd_y, second, first),
            )
        result = []
        for plane in range(3):
            at = row if row < 3 else row - 7
            first, second = x1[at, plane].astype(F32), x2[at, plane].astype(F32)
            if row < 3:
                result.append(jnp.where(odd_x, first, second))
            else:
                result.append(jnp.where(odd_x, second, first))
        return result

    fill_deep(10, gx * 4 - 3, planes, stacked)
    deep_conv(8, stacked, weight, out)


def second_kernel(own, y1, y2, weight, out, stacked):
    gx, gy = lax.axis_index("gx"), lax.axis_index("gy")
    odd_y = lax.rem(gy, 2) == 1

    def planes(row):
        first, second = y1[row].astype(F32), y2[row].astype(F32)
        return (
            jnp.where(odd_y, first, second),
            own[row].astype(F32),
            jnp.where(odd_y, second, first),
        )

    fill_deep(8, gx * 4 - 2, planes, stacked)
    deep_conv(6, stacked, weight, out)


def decode_kernel(
    own, y1, y2, encoded, ex1, ex2, ey1, ey2, up, weight, decoded, stacked, upward
):
    gx, gy = lax.axis_index("gx"), lax.axis_index("gy")
    odd_x, odd_y = lax.rem(gx, 2) == 1, lax.rem(gy, 2) == 1
    nx, ny = lax.axis_size("gx"), lax.axis_size("gy")

    low = jnp.where(odd_y, y1[...].astype(F32), y2[...].astype(F32)).astype(BF).reshape(192, 256)
    high = jnp.where(odd_y, y2[...].astype(F32), y1[...].astype(F32)).astype(BF).reshape(192, 256)
    mid = own[...].reshape(192, 256)
    for col, (cells, b) in enumerate(((low, 1), (mid, 0), (mid, 1), (high, 0))):
        for a in range(2):
            for d in range(2):
                part = leaky_unit(
                    jnp.dot(cells, up[a, b, d], preferred_element_type=F32)
                ).reshape(6, 32, 128)
                for i in range(6):
                    row = 2 * i + a - 1
                    if 0 <= row < 10:
                        upward[row, col, pl.ds(d, 32, stride=2), :] = part[i]

    def put(row, col, half, cells):
        for tap, part in enumerate(depth_taps(cells)):
            lane = (col * 3 + tap) * 256 + half * 128
            stacked[row, :, lane : lane + 128] = part

    def one_row(row, carry):
        ok_row = inside(gx * 8 - 1 + row, nx * 8)
        for col in range(4):
            ok = ok_row & inside(gy * 2 - 1 + col, ny * 2)
            put(row, col, 0, jnp.where(ok, upward[row, col], 0.0))
        first, second = ey1[row].astype(F32), ey2[row].astype(F32)
        put(row, 0, 1, jnp.where(ok_row & (gy > 0), jnp.where(odd_y, first, second), 0.0))
        put(row, 3, 1, jnp.where(ok_row & (gy < ny - 1), jnp.where(odd_y, second, first), 0.0))
        return carry

    lax.fori_loop(0, 10, one_row, 0)

    def center(row, carry):
        put(row + 1, 1, 1, encoded[row, 0].astype(F32))
        put(row + 1, 2, 1, encoded[row, 1].astype(F32))
        return carry

    lax.fori_loop(0, 8, center, 0)
    for col in range(2):
        first, second = ex1[col].astype(F32), ex2[col].astype(F32)
        put(0, col + 1, 1, jnp.where(gx > 0, jnp.where(odd_x, first, second), 0.0))
        put(9, col + 1, 1, jnp.where(gx < nx - 1, jnp.where(odd_x, second, first), 0.0))

    total = jnp.zeros((512, 256), F32)
    for off in range(3):
        total = total + jnp.dot(
            stacked[off : off + 8].reshape(512, 3072), weight[off], preferred_element_type=F32
        )
    result = leaky_unit(total).astype(BF).reshape(8, 64, 256)
    decoded[:, 0] = result[:, :, :128]
    decoded[:, 1] = result[:, :, 128:]


def call(kernel, outs, scratch, name, flops, *operands):
    vmem = pl.BlockSpec(memory_space=pltpu.VMEM)
    return pl.pallas_call(
        kernel,
        out_shape=[jax.ShapeDtypeStruct(shape, BF) for shape in outs],
        in_specs=[vmem] * len(operands),
        out_specs=[vmem] * len(outs),
        scratch_shapes=[pltpu.VMEM(shape, dtype) for shape, dtype in scratch],
        compiler_params=pltpu.CompilerParams(vmem_limit_bytes=LIMIT),
        cost_estimate=pl.CostEstimate(flops=flops, bytes_accessed=4 << 20, transcendentals=0),
        name=name,
    )(*operands)


def pair_columns(weight):
    depth = 3 * weight.shape[3]
    flat = weight.reshape(3, 3 * depth, 128)
    first = jnp.pad(flat, ((0, 0), (0, depth), (0, 0)))
    second = jnp.pad(flat, ((0, 0), (depth, 0), (0, 0)))
    return jnp.concatenate([first, second], axis=2)


def near(count):
    return [(i, i ^ 1) for i in range(count)]


def far(count):
    return [(i, (((i + 1) ^ 1) - 1) % count) for i in range(count)]


def swap_y(first, second):
    count = lax.axis_size("gy")
    return lax.ppermute(first, "gy", near(count)), lax.ppermute(second, "gy", far(count))


def swap_x(first, second):
    count = lax.axis_size("gx")
    return lax.ppermute(first, "gx", near(count)), lax.ppermute(second, "gx", far(count))


def local(
    volume,
    weight_entry,
    weight_down,
    weight_deep_first,
    weight_deep_second,
    weight_upward,
    weight_decoder,
):
    odd_x = lax.rem(lax.axis_index("gx"), 2)
    odd_y = lax.rem(lax.axis_index("gy"), 2)

    def column(array, at):
        return lax.dynamic_index_in_dim(array, at, axis=1, keepdims=False)

    def rows(array, at, count):
        return lax.dynamic_slice_in_dim(array, at, count, axis=0)

    y1, y2 = swap_y(column(volume, 1 - odd_y), column(volume, odd_y))
    low = jnp.where(odd_y == 1, y1, y2)
    high = jnp.where(odd_y == 1, y2, y1)

    def edge(at):
        return jnp.concatenate(
            [rows(low, at, 1), rows(volume, at, 1)[0], rows(high, at, 1)], axis=0
        )

    x1, x2 = swap_x(edge(7 * (1 - odd_x)), edge(7 * odd_x))
    encoded, coarse = call(
        entry_kernel,
        [(8, 2, 64, 128), (4, 32, 256)],
        [((10, 64, 1536), BF), ((8, 2, 64, 128), F32)],
        "entry",
        1_300_000_000,
        volume,
        y1,
        y2,
        x1,
        x2,
        pair_columns(weight_entry),
        weight_down,
    )

    c1, c2 = swap_y(coarse, coarse)
    c_low = jnp.where(odd_y == 1, c1, c2)
    c_high = jnp.where(odd_y == 1, c2, c1)

    def coarse_edge(at):
        return jnp.stack([rows(c_low, at, 3), rows(coarse, at, 3), rows(c_high, at, 3)], axis=1)

    d1, d2 = swap_x(coarse_edge(1 - odd_x), coarse_edge(odd_x))
    e1, e2 = swap_x(rows(encoded, 7 * (1 - odd_x), 1)[0], rows(encoded, 7 * odd_x, 1)[0])
    (deep_one,) = call(
        first_kernel,
        [(8, 32, 256)],
        [((10, 32, 2304), BF)],
        "first",
        1_000_000_000,
        coarse,
        c1,
        c2,
        d1,
        d2,
        weight_deep_first.reshape(3, 2304, 256),
    )
    f1, f2 = swap_y(deep_one, deep_one)

    e_low = jnp.where(odd_x == 1, e1, e2)
    e_high = jnp.where(odd_x == 1, e2, e1)

    def encoded_edge(at):
        return jnp.concatenate(
            [rows(e_low, at, 1), column(encoded, at), rows(e_high, at, 1)], axis=0
        )

    g1, g2 = swap_y(encoded_edge(1 - odd_y), encoded_edge(odd_y))
    (deep_two,) = call(
        second_kernel,
        [(6, 32, 256)],
        [((8, 32, 2304), BF)],
        "second",
        700_000_000,
        deep_one,
        f1,
        f2,
        weight_deep_second.reshape(3, 2304, 256),
    )
    h1, h2 = swap_y(deep_two, deep_two)
    (decoded,) = call(
        decode_kernel,
        [(8, 2, 64, 128)],
        [((10, 64, 3072), BF), ((10, 4, 64, 128), F32)],
        "decode",
        2_700_000_000,
        deep_two,
        h1,
        h2,
        encoded,
        e1,
        e2,
        g1,
        g2,
        weight_upward,
        pair_columns(weight_decoder),
    )
    return decoded


def solution(mesh):
    return jax.shard_map(
        local,
        mesh=mesh,
        in_specs=(P("gx", "gy", None, None), P(), P(), P(), P(), P(), P()),
        out_specs=P("gx", "gy", None, None),
        check_vma=False,
    )
```

```python
import jax
import jax.numpy as jnp
from jax import lax
from jax.experimental import pallas as pl
from jax.experimental.pallas import tpu as pltpu
from jax.sharding import PartitionSpec as P

BF = jnp.bfloat16
F32 = jnp.float32
LIMIT = 20 * 1024 * 1024


def leaky_unit(values):
    return jnp.where(values > 0, values, 0.1 * values)


def inside(index, count):
    return (index >= 0) & (index < count)


def depth_taps(cells):
    depth = cells.shape[0]
    at = lax.broadcasted_iota(jnp.int32, cells.shape, 0)
    before = jnp.where(at == 0, 0.0, pltpu.roll(cells, 1, axis=0))
    after = jnp.where(at == depth - 1, 0.0, pltpu.roll(cells, depth - 1, axis=0))
    return before.astype(BF), cells.astype(BF), after.astype(BF)


def own_columns(target, part):
    for off in range(3):
        target[off, :384, :128] = part(off, 1)
        target[off, :384, 128:] = part(off, 0)
        target[off, 384:, :128] = part(off, 2)
        target[off, 384:, 128:] = part(off, 1)


def put_taps(target, row, lane, cells):
    for tap, part in enumerate(depth_taps(cells)):
        target[row, :, lane + tap * 128 : lane + tap * 128 + 128] = part


def side_columns(total, rows, low, high, part):
    extra = low.shape[0] - 8
    for off in range(3):
        if extra == 2:
            source, into = slice(off, off + 8), slice(0, 8)
        else:
            source = slice(max(0, off - 1), 8 + min(0, off - 1))
            into = slice(max(0, 1 - off), 8 - max(0, off - 1))
        count = (into.stop - into.start) * 64
        for half, cells in enumerate((low, high)):
            lanes = slice(half * 128, half * 128 + 128)
            total[into, :, lanes] += jnp.dot(
                cells[source].reshape(count, 384), part(off, 2 * half), preferred_element_type=F32
            ).reshape(count // 64, 64, 128)


def entry_own_kernel(own, weight, total, stacked, wide):
    own_columns(wide, lambda off, col: weight[off, col])

    def one_row(i, carry):
        for col in range(2):
            put_taps(stacked, i, col * 384, own[i, col].astype(F32))
        return carry

    lax.fori_loop(0, 8, one_row, 0)
    total[...] = jnp.dot(
        stacked[...].reshape(512, 768), wide[1], preferred_element_type=F32
    ).reshape(8, 64, 256)
    total[1:8] += jnp.dot(
        stacked[0:7].reshape(448, 768), wide[0], preferred_element_type=F32
    ).reshape(7, 64, 256)
    total[0:7] += jnp.dot(
        stacked[1:8].reshape(448, 768), wide[2], preferred_element_type=F32
    ).reshape(7, 64, 256)


def entry_side_kernel(y1, y2, weight, before, total, low, high):
    gy = lax.axis_index("gy")
    ny = lax.axis_size("gy")
    odd_y = lax.rem(gy, 2) == 1
    total[...] = before[...]

    def one_row(i, carry):
        first, second = y1[i].astype(F32), y2[i].astype(F32)
        put_taps(low, i, 0, jnp.where(gy > 0, jnp.where(odd_y, first, second), 0.0))
        put_taps(high, i, 0, jnp.where(gy < ny - 1, jnp.where(odd_y, second, first), 0.0))
        return carry

    lax.fori_loop(0, 8, one_row, 0)
    side_columns(total, 8, low, high, lambda off, col: weight[off, col])


def entry_last_kernel(x1, x2, weight, down, before, encoded, coarse, stacked, fine):
    gx, gy = lax.axis_index("gx"), lax.axis_index("gy")
    nx, ny = lax.axis_size("gx"), lax.axis_size("gy")
    odd_x = lax.rem(gx, 2) == 1
    for col in range(4):
        first, second = x1[col].astype(F32), x2[col].astype(F32)
        low = jnp.where(odd_x, first, second)
        high = jnp.where(odd_x, second, first)
        ok = inside(gy * 2 - 1 + col, ny * 2)
        put_taps(stacked, 0, col * 384, jnp.where(ok & (gx > 0), low, 0.0))
        put_taps(stacked, 1, col * 384, jnp.where(ok & (gx < nx - 1), high, 0.0))

    def finish(row, values):
        result = leaky_unit(values).astype(BF)
        for b in range(2):
            half = result[..., b * 128 : b * 128 + 128]
            encoded[row, b] = half
            fine[row, b] = half.astype(F32)

    def middle(row, carry):
        finish(row, before[row])
        return carry

    lax.fori_loop(1, 7, middle, 0)
    for side, (row, off) in enumerate(((0, 0), (7, 2))):
        extra = [
            jnp.dot(
                stacked[side, :, b * 384 : b * 384 + 1152],
                weight[off].reshape(1152, 128),
                preferred_element_type=F32,
            )
            for b in range(2)
        ]
        finish(row, before[row] + jnp.concatenate(extra, axis=1))
    small = jnp.zeros((128, 256), F32)
    for a in range(2):
        for d in range(2):
            cells = jnp.concatenate(
                [
                    jnp.concatenate(
                        [fine[2 * i + a, b, pl.ds(d, 32, stride=2), :] for b in range(2)], axis=1
                    )
                    for i in range(4)
                ],
                axis=0,
            ).astype(BF)
            small = small + jnp.dot(
                cells, down[a, :, d].reshape(256, 256), preferred_element_type=F32
            )
    coarse[...] = leaky_unit(small).astype(BF).reshape(4, 32, 256)


def fill_deep(rows, first_row, planes, stacked):
    gy = lax.axis_index("gy")
    nx, ny = lax.axis_size("gx"), lax.axis_size("gy")

    for row in range(rows):
        ok_row = inside(first_row + row, nx * 4)
        for plane, cells in enumerate(planes(row)):
            ok = ok_row & inside(gy - 1 + plane, ny)
            for tap, part in enumerate(depth_taps(jnp.where(ok, cells, 0.0))):
                lane = (plane * 3 + tap) * 256
                stacked[row, :, lane : lane + 256] = part


def deep_conv(rows, stacked, weight, out):
    total = jnp.zeros((rows * 32, 256), F32)
    for off in range(3):
        total = total + jnp.dot(
            stacked[off : off + rows].reshape(rows * 32, 2304),
            weight[off],
            preferred_element_type=F32,
        )
    out[...] = leaky_unit(total).astype(BF).reshape(rows, 32, 256)


def first_kernel(own, y1, y2, x1, x2, weight, out, stacked):
    gx, gy = lax.axis_index("gx"), lax.axis_index("gy")
    odd_x, odd_y = lax.rem(gx, 2) == 1, lax.rem(gy, 2) == 1

    def planes(row):
        if 3 <= row < 7:
            first, second = y1[row - 3].astype(F32), y2[row - 3].astype(F32)
            return (
                jnp.where(odd_y, first, second),
                own[row - 3].astype(F32),
                jnp.where(odd_y, second, first),
            )
        result = []
        for plane in range(3):
            at = row if row < 3 else row - 7
            first, second = x1[at, plane].astype(F32), x2[at, plane].astype(F32)
            if row < 3:
                result.append(jnp.where(odd_x, first, second))
            else:
                result.append(jnp.where(odd_x, second, first))
        return result

    fill_deep(10, gx * 4 - 3, planes, stacked)
    deep_conv(8, stacked, weight, out)


def second_kernel(own, y1, y2, weight, out, stacked):
    gx, gy = lax.axis_index("gx"), lax.axis_index("gy")
    odd_y = lax.rem(gy, 2) == 1

    def planes(row):
        first, second = y1[row].astype(F32), y2[row].astype(F32)
        return (
            jnp.where(odd_y, first, second),
            own[row].astype(F32),
            jnp.where(odd_y, second, first),
        )

    fill_deep(8, gx * 4 - 2, planes, stacked)
    deep_conv(6, stacked, weight, out)


def lift(cells, up, upward, columns):
    for col, b in columns:
        for a in range(2):
            for d in range(2):
                part = leaky_unit(
                    jnp.dot(cells, up[a, b, d], preferred_element_type=F32)
                ).reshape(6, 32, 128)
                for i in range(6):
                    row = 2 * i + a - 1
                    if 0 <= row < 10:
                        upward[row, col, pl.ds(d, 32, stride=2), :] = part[i]


def decode_own_kernel(
    own, encoded, ex1, ex2, ey1, ey2, up, weight, total, stacked, low, high, wide, upward
):
    gx, gy = lax.axis_index("gx"), lax.axis_index("gy")
    nx, ny = lax.axis_size("gx"), lax.axis_size("gy")
    odd_x, odd_y = lax.rem(gx, 2) == 1, lax.rem(gy, 2) == 1

    def weights(half):
        return lambda off, col: weight[off, col, :, half * 128 : half * 128 + 128].reshape(
            384, 128
        )

    own_columns(wide, weights(1))

    def side(row, carry):
        ok = inside(gx * 8 - 1 + row, nx * 8)
        first, second = ey1[row].astype(F32), ey2[row].astype(F32)
        put_taps(low, row, 0, jnp.where(ok & (gy > 0), jnp.where(odd_y, first, second), 0.0))
        put_taps(high, row, 0, jnp.where(ok & (gy < ny - 1), jnp.where(odd_y, second, first), 0.0))
        return carry

    lax.fori_loop(0, 10, side, 0)

    def center(row, carry):
        for col in range(2):
            put_taps(stacked, row + 1, col * 384, encoded[row, col].astype(F32))
        return carry

    lax.fori_loop(0, 8, center, 0)
    for col in range(2):
        first, second = ex1[col].astype(F32), ex2[col].astype(F32)
        lane = col * 384
        put_taps(stacked, 0, lane, jnp.where(gx > 0, jnp.where(odd_x, first, second), 0.0))
        put_taps(stacked, 9, lane, jnp.where(gx < nx - 1, jnp.where(odd_x, second, first), 0.0))

    def add_own(start):
        for off in range(3):
            part = jnp.dot(
                stacked[off : off + 8].reshape(512, 768), wide[off], preferred_element_type=F32
            ).reshape(8, 64, 256)
            if start and off == 0:
                total[...] = part
            else:
                total[...] += part

    add_own(True)
    side_columns(total, 10, low, high, weights(1))
    own_columns(wide, weights(0))
    lift(own[...].reshape(192, 256), up, upward, ((0, 0), (1, 1)))

    def lifted(row, carry):
        ok = inside(gx * 8 - 1 + row, nx * 8)
        for col in range(2):
            put_taps(stacked, row, col * 384, jnp.where(ok, upward[row, col], 0.0))
        return carry

    lax.fori_loop(0, 10, lifted, 0)
    add_own(False)


def decode_last_kernel(y1, y2, up, weight, before, decoded, low, high, upward, total):
    gx, gy = lax.axis_index("gx"), lax.axis_index("gy")
    nx, ny = lax.axis_size("gx"), lax.axis_size("gy")
    odd_y = lax.rem(gy, 2) == 1
    total[...] = before[...]
    first, second = y1[...].astype(F32), y2[...].astype(F32)
    below = jnp.where(odd_y, first, second).astype(BF).reshape(192, 256)
    above = jnp.where(odd_y, second, first).astype(BF).reshape(192, 256)
    lift(below, up, upward, ((0, 1),))
    lift(above, up, upward, ((1, 0),))

    def lifted(row, carry):
        ok = inside(gx * 8 - 1 + row, nx * 8)
        put_taps(low, row, 0, jnp.where(ok & (gy > 0), upward[row, 0], 0.0))
        put_taps(high, row, 0, jnp.where(ok & (gy < ny - 1), upward[row, 1], 0.0))
        return carry

    lax.fori_loop(0, 10, lifted, 0)
    side_columns(
        total, 10, low, high, lambda off, col: weight[off, col, :, :128].reshape(384, 128)
    )
    result = leaky_unit(total[...]).astype(BF)
    decoded[:, 0] = result[:, :, :128]
    decoded[:, 1] = result[:, :, 128:]


def call(kernel, outs, scratch, name, flops, *operands):
    vmem = pl.BlockSpec(memory_space=pltpu.VMEM)
    return pl.pallas_call(
        kernel,
        out_shape=[jax.ShapeDtypeStruct(shape, dtype) for shape, dtype in outs],
        in_specs=[vmem] * len(operands),
        out_specs=[vmem] * len(outs),
        scratch_shapes=[pltpu.VMEM(shape, dtype) for shape, dtype in scratch],
        compiler_params=pltpu.CompilerParams(vmem_limit_bytes=LIMIT),
        cost_estimate=pl.CostEstimate(flops=flops, bytes_accessed=1 << 20, transcendentals=0),
        name=name,
    )(*operands)


def swap_y(first, second):
    nx, ny = lax.axis_size("gx"), lax.axis_size("gy")
    near = [(i, i ^ 1) for i in range(ny)]
    far = []
    for x in range(nx):
        for y in range(ny):
            to = (x ^ 1) * ny + y if y in (0, ny - 1) else x * ny + ((y + 1) ^ 1) - 1
            far.append((x * ny + y, to))
    got = lax.ppermute(second, ("gx", "gy"), far)
    return lax.ppermute(first, "gy", near), got


def swap_x(first, second):
    nx, ny = lax.axis_size("gx"), lax.axis_size("gy")
    near = [(i, i ^ 1) for i in range(nx)]
    far = []
    for x in range(nx):
        for y in range(ny):
            to = x * ny + (y ^ 1) if x in (0, nx - 1) else (((x + 1) ^ 1) - 1) * ny + y
            far.append((x * ny + y, to))
    got = lax.ppermute(second, ("gx", "gy"), far)
    return lax.ppermute(first, "gx", near), got


def local(
    volume,
    weight_entry,
    weight_down,
    weight_deep_first,
    weight_deep_second,
    weight_upward,
    weight_decoder,
):
    odd_x = lax.rem(lax.axis_index("gx"), 2)
    odd_y = lax.rem(lax.axis_index("gy"), 2)

    def column(array, at):
        return lax.dynamic_index_in_dim(array, at, axis=1, keepdims=False)

    def rows(array, at, count):
        return lax.dynamic_slice_in_dim(array, at, count, axis=0)

    entry = weight_entry.reshape(3, 3, 384, 128)
    sums = ((8, 64, 256), F32)
    y1, y2 = swap_y(column(volume, 1 - odd_y), column(volume, odd_y))
    (total,) = call(
        entry_own_kernel,
        [sums],
        [((8, 64, 768), BF), ((3, 768, 256), BF)],
        "entry_own",
        2_000_000_000,
        volume,
        entry,
    )
    low = jnp.where(odd_y == 1, y1, y2)
    high = jnp.where(odd_y == 1, y2, y1)

    def edge(at):
        return jnp.concatenate(
            [rows(low, at, 1), rows(volume, at, 1)[0], rows(high, at, 1)], axis=0
        )

    x1, x2 = swap_x(edge(7 * (1 - odd_x)), edge(7 * odd_x))
    (total,) = call(
        entry_side_kernel,
        [sums],
        [((8, 64, 384), BF), ((8, 64, 384), BF)],
        "entry_side",
        1_000_000_000,
        y1,
        y2,
        entry,
        total,
    )
    encoded, coarse = call(
        entry_last_kernel,
        [((8, 2, 64, 128), BF), ((4, 32, 256), BF)],
        [((2, 64, 1536), BF), ((8, 2, 64, 128), F32)],
        "entry_last",
        1_000_000_000,
        x1,
        x2,
        entry,
        weight_down,
        total,
    )

    c1, c2 = swap_y(coarse, coarse)
    c_low = jnp.where(odd_y == 1, c1, c2)
    c_high = jnp.where(odd_y == 1, c2, c1)

    def coarse_edge(at):
        return jnp.stack([rows(c_low, at, 3), rows(coarse, at, 3), rows(c_high, at, 3)], axis=1)

    d1, d2 = swap_x(coarse_edge(1 - odd_x), coarse_edge(odd_x))
    e1, e2 = swap_x(rows(encoded, 7 * (1 - odd_x), 1)[0], rows(encoded, 7 * odd_x, 1)[0])
    (deep_one,) = call(
        first_kernel,
        [((8, 32, 256), BF)],
        [((10, 32, 2304), BF)],
        "first",
        1_000_000_000,
        coarse,
        c1,
        c2,
        d1,
        d2,
        weight_deep_first.reshape(3, 2304, 256),
    )
    f1, f2 = swap_y(deep_one, deep_one)

    e_low = jnp.where(odd_x == 1, e1, e2)
    e_high = jnp.where(odd_x == 1, e2, e1)

    def encoded_edge(at):
        return jnp.concatenate(
            [rows(e_low, at, 1), column(encoded, at), rows(e_high, at, 1)], axis=0
        )

    g1, g2 = swap_y(encoded_edge(1 - odd_y), encoded_edge(odd_y))
    (deep_two,) = call(
        second_kernel,
        [((6, 32, 256), BF)],
        [((8, 32, 2304), BF)],
        "second",
        700_000_000,
        deep_one,
        f1,
        f2,
        weight_deep_second.reshape(3, 2304, 256),
    )
    h1, h2 = swap_y(deep_two, deep_two)
    (total,) = call(
        decode_own_kernel,
        [sums],
        [
            ((10, 64, 768), BF),
            ((10, 64, 384), BF),
            ((10, 64, 384), BF),
            ((3, 768, 256), BF),
            ((10, 2, 64, 128), F32),
        ],
        "decode_own",
        3_000_000_000,
        deep_two,
        encoded,
        e1,
        e2,
        g1,
        g2,
        weight_upward,
        weight_decoder,
    )
    (decoded,) = call(
        decode_last_kernel,
        [((8, 2, 64, 128), BF)],
        [
            ((10, 64, 384), BF),
            ((10, 64, 384), BF),
            ((10, 2, 64, 128), F32),
            ((8, 64, 256), F32),
        ],
        "decode_last",
        1_000_000_000,
        h1,
        h2,
        weight_upward,
        weight_decoder,
        total,
    )
    return decoded


def solution(mesh):
    return jax.shard_map(
        local,
        mesh=mesh,
        in_specs=(P("gx", "gy", None, None), P(), P(), P(), P(), P(), P()),
        out_specs=P("gx", "gy", None, None),
        check_vma=False,
    )
```

```python
import jax
import jax.numpy as jnp
from jax import lax
from jax.experimental import pallas as pl
from jax.experimental.pallas import tpu as pltpu
from jax.sharding import PartitionSpec as P

BF = jnp.bfloat16
F32 = jnp.float32
LIMIT = 20 * 1024 * 1024


def leaky_unit(values):
    return jnp.where(values > 0, values, 0.1 * values)


def inside(index, count):
    return (index >= 0) & (index < count)


def depth_taps(cells):
    depth = cells.shape[0]
    at = lax.broadcasted_iota(jnp.int32, cells.shape, 0)
    before = jnp.where(at == 0, 0.0, pltpu.roll(cells, 1, axis=0))
    after = jnp.where(at == depth - 1, 0.0, pltpu.roll(cells, depth - 1, axis=0))
    return before.astype(BF), cells.astype(BF), after.astype(BF)


def own_columns(target, part):
    for off in range(3):
        target[off, :384, :128] = part(off, 1)
        target[off, :384, 128:] = part(off, 0)
        target[off, 384:, :128] = part(off, 2)
        target[off, 384:, 128:] = part(off, 1)


def put_taps(target, row, lane, cells):
    for tap, part in enumerate(depth_taps(cells)):
        target[row, :, lane + tap * 128 : lane + tap * 128 + 128] = part


def spans(cells, off):
    if cells.shape[0] == 10:
        return slice(off, off + 8), slice(0, 8)
    return slice(max(0, off - 1), min(8, 7 + off)), slice(max(0, 1 - off), min(8, 9 - off))


def add_own(total, cells, wide, start=False):
    for off in (1, 0, 2):
        source, into = spans(cells, off)
        rows = into.stop - into.start
        part = jnp.dot(
            cells[source].reshape(rows * 64, 768), wide[off], preferred_element_type=F32
        ).reshape(rows, 64, 256)
        for b in range(2):
            half = part[:, :, b * 128 : b * 128 + 128]
            if start and off == 1:
                total[b] = half
            else:
                total[b, into] += half


def add_side(total, cells, part, side):
    for off in (1, 0, 2):
        source, into = spans(cells, off)
        rows = into.stop - into.start
        total[side, into] += jnp.dot(
            cells[source].reshape(rows * 64, 384), part(off, 2 * side), preferred_element_type=F32
        ).reshape(rows, 64, 128)


def add_rows(total, x_near, x_far, stacked, part):
    gx, gy = lax.axis_index("gx"), lax.axis_index("gy")
    nx, ny = lax.axis_size("gx"), lax.axis_size("gy")
    odd_x = lax.rem(gx, 2) == 1
    for col in range(4):
        first, second = x_near[col].astype(F32), x_far[col].astype(F32)
        low = jnp.where(odd_x, first, second)
        high = jnp.where(odd_x, second, first)
        ok = inside(gy * 2 - 1 + col, ny * 2)
        put_taps(stacked, 0, col * 384, jnp.where(ok & (gx > 0), low, 0.0))
        put_taps(stacked, 1, col * 384, jnp.where(ok & (gx < nx - 1), high, 0.0))
    for side, (row, off) in enumerate(((0, 0), (7, 2))):
        for b in range(2):
            total[b, row] += jnp.dot(
                stacked[side, :, b * 384 : b * 384 + 1152],
                part(off).reshape(1152, 128),
                preferred_element_type=F32,
            )


def sides():
    gy = lax.axis_index("gy")
    odd = lax.rem(gy, 2)
    return 1 - odd, odd, (gy > 0) & (gy < lax.axis_size("gy") - 1)


def prep_kernel(volume, own, near, far, edge_near, edge_far, sem):
    copy = pltpu.make_async_copy(volume, own, sem)
    copy.start()
    odd_x, odd_y = lax.rem(lax.axis_index("gx"), 2), lax.rem(lax.axis_index("gy"), 2)
    copy.wait()
    near[...] = own[:, 1 - odd_y]
    far[...] = own[:, odd_y]
    edge_near[...] = own[7 * (1 - odd_x)]
    edge_far[...] = own[7 * odd_x]


def entry_own_kernel(own, weight_hbm, total, weight, stacked, wide, sem):
    copy = pltpu.make_async_copy(weight_hbm, weight, sem)
    copy.start()

    def one_row(i, carry):
        for col in range(2):
            put_taps(stacked, i, col * 384, own[i, col].astype(F32))
        return carry

    lax.fori_loop(0, 8, one_row, 0)
    copy.wait()
    own_columns(wide, lambda off, col: weight[off, col])
    add_own(total, stacked, wide, start=True)


def entry_side_kernel(y_near, y_far, weight, before, total, near, far):
    side_near, side_far, far_ok = sides()
    total[...] = before[...]

    def one_row(i, carry):
        put_taps(near, i, 0, y_near[i].astype(F32))
        put_taps(far, i, 0, jnp.where(far_ok, y_far[i].astype(F32), 0.0))
        return carry

    lax.fori_loop(0, 8, one_row, 0)
    add_side(total, near, lambda off, col: weight[off, col], side_near)
    add_side(total, far, lambda off, col: weight[off, col], side_far)


def entry_last_kernel(x_near, x_far, weight, down, before, encoded, coarse, stacked, fine, total):
    total[:, 0] = before[:, 0]
    total[:, 7] = before[:, 7]
    add_rows(total, x_near, x_far, stacked, lambda off: weight[off])

    def finish(row, source):
        for b in range(2):
            half = leaky_unit(source[b, row]).astype(BF)
            encoded[row, b] = half
            fine[row, b] = half.astype(F32)

    def middle(row, carry):
        finish(row, before)
        return carry

    lax.fori_loop(1, 7, middle, 0)
    finish(0, total)
    finish(7, total)
    small = jnp.zeros((128, 256), F32)
    for a in range(2):
        for d in range(2):
            cells = jnp.concatenate(
                [
                    jnp.concatenate(
                        [fine[2 * i + a, b, pl.ds(d, 32, stride=2), :] for b in range(2)], axis=1
                    )
                    for i in range(4)
                ],
                axis=0,
            ).astype(BF)
            small = small + jnp.dot(
                cells, down[a, :, d].reshape(256, 256), preferred_element_type=F32
            )
    coarse[...] = leaky_unit(small).astype(BF).reshape(4, 32, 256)


def fill_deep(rows, first_row, planes, stacked):
    gy = lax.axis_index("gy")
    nx, ny = lax.axis_size("gx"), lax.axis_size("gy")

    for row in range(rows):
        ok_row = inside(first_row + row, nx * 4)
        for plane, cells in enumerate(planes(row)):
            ok = ok_row & inside(gy - 1 + plane, ny)
            for tap, part in enumerate(depth_taps(jnp.where(ok, cells, 0.0))):
                lane = (plane * 3 + tap) * 256
                stacked[row, :, lane : lane + 256] = part


def deep_conv(rows, stacked, weight, out):
    total = jnp.zeros((rows * 32, 256), F32)
    for off in range(3):
        total = total + jnp.dot(
            stacked[off : off + rows].reshape(rows * 32, 2304),
            weight[off],
            preferred_element_type=F32,
        )
    out[...] = leaky_unit(total).astype(BF).reshape(rows, 32, 256)


def first_kernel(own, y1, y2, x1, x2, weight, out, stacked):
    gx, gy = lax.axis_index("gx"), lax.axis_index("gy")
    odd_x, odd_y = lax.rem(gx, 2) == 1, lax.rem(gy, 2) == 1

    def planes(row):
        if 3 <= row < 7:
            first, second = y1[row - 3].astype(F32), y2[row - 3].astype(F32)
            return (
                jnp.where(odd_y, first, second),
                own[row - 3].astype(F32),
                jnp.where(odd_y, second, first),
            )
        result = []
        for plane in range(3):
            at = row if row < 3 else row - 7
            first, second = x1[at, plane].astype(F32), x2[at, plane].astype(F32)
            if row < 3:
                result.append(jnp.where(odd_x, first, second))
            else:
                result.append(jnp.where(odd_x, second, first))
        return result

    fill_deep(10, gx * 4 - 3, planes, stacked)
    deep_conv(8, stacked, weight, out)


def second_kernel(own, y1, y2, weight, out, stacked):
    gx, gy = lax.axis_index("gx"), lax.axis_index("gy")
    odd_y = lax.rem(gy, 2) == 1

    def planes(row):
        first, second = y1[row].astype(F32), y2[row].astype(F32)
        return (
            jnp.where(odd_y, first, second),
            own[row].astype(F32),
            jnp.where(odd_y, second, first),
        )

    fill_deep(8, gx * 4 - 2, planes, stacked)
    deep_conv(6, stacked, weight, out)


def half_weights(weight, half):
    return lambda off, col: weight[off, col, :, half * 128 : half * 128 + 128].reshape(384, 128)


def lift(cells, up, b, upward, col):
    for a in range(2):
        for d in range(2):
            part = leaky_unit(jnp.dot(cells, up[a, b, d], preferred_element_type=F32))
            part = part.reshape(6, 32, 128)
            for i in range(6):
                row = 2 * i + a - 1
                if 0 <= row < 10:
                    upward[row, col, pl.ds(d, 32, stride=2), :] = part[i]


def put_lifted(target, upward, cols, y_ok):
    gx, nx = lax.axis_index("gx"), lax.axis_size("gx")

    def lifted(row, carry):
        ok = y_ok & inside(gx * 8 - 1 + row, nx * 8)
        for col in range(cols):
            put_taps(target, row, col * 384, jnp.where(ok, upward[row, col], 0.0))
        return carry

    lax.fori_loop(0, 10, lifted, 0)


def decode_skip_kernel(encoded, y_near, y_far, weight, total, stacked, near, far, wide):
    side_near, side_far, far_ok = sides()
    part = half_weights(weight, 1)
    own_columns(wide, part)

    def one_row(i, carry):
        for col in range(2):
            put_taps(stacked, i, col * 384, encoded[i, col].astype(F32))
        put_taps(near, i, 0, y_near[i].astype(F32))
        put_taps(far, i, 0, jnp.where(far_ok, y_far[i].astype(F32), 0.0))
        return carry

    lax.fori_loop(0, 8, one_row, 0)
    add_own(total, stacked, wide, start=True)
    add_side(total, near, part, side_near)
    add_side(total, far, part, side_far)


def decode_own_kernel(
    own, x_near, x_far, up, weight, before, total, stacked, edges, wide, upward
):
    total[...] = before[...]
    part = half_weights(weight, 0)
    own_columns(wide, part)
    lift(own[...].reshape(192, 256), up, 0, upward, 0)
    lift(own[...].reshape(192, 256), up, 1, upward, 1)
    put_lifted(stacked, upward, 2, True)
    add_own(total, stacked, wide)
    add_rows(total, x_near, x_far, edges, lambda off: weight[off, :, :, 128:])


def decode_near_kernel(y_near, up, weight, before, total, near, upward):
    side, _, _ = sides()
    total[...] = before[...]
    lift(y_near[...].reshape(192, 256), up, 1 - side, upward, 0)
    put_lifted(near, upward, 1, True)
    add_side(total, near, half_weights(weight, 0), side)


def decode_last_kernel(y_far, up, weight, before, decoded, far, upward, total):
    _, side, far_ok = sides()
    total[...] = before[...]
    lift(y_far[...].reshape(192, 256), up, 1 - side, upward, 0)
    put_lifted(far, upward, 1, far_ok)
    add_side(total, far, half_weights(weight, 0), side)
    for b in range(2):
        decoded[:, b] = leaky_unit(total[b]).astype(BF)


def call(kernel, outs, scratch, name, flops, *operands, remote=()):
    vmem = pl.BlockSpec(memory_space=pltpu.VMEM)
    anywhere = pl.BlockSpec(memory_space=pltpu.HBM)
    return pl.pallas_call(
        kernel,
        out_shape=[jax.ShapeDtypeStruct(shape, dtype) for shape, dtype in outs],
        in_specs=[anywhere if i in remote else vmem for i in range(len(operands))],
        out_specs=[vmem] * len(outs),
        scratch_shapes=[
            pltpu.SemaphoreType.DMA if shape is None else pltpu.VMEM(shape, dtype)
            for shape, dtype in scratch
        ],
        compiler_params=pltpu.CompilerParams(vmem_limit_bytes=LIMIT),
        cost_estimate=pl.CostEstimate(flops=flops, bytes_accessed=1 << 20, transcendentals=0),
        name=name,
    )(*operands)


def swap_y(near_cells, far_cells, far_first=True):
    nx, ny = lax.axis_size("gx"), lax.axis_size("gy")
    near = [(i, i ^ 1) for i in range(ny)]
    far = []
    for x in range(nx):
        for y in range(ny):
            to = (x ^ 1) * ny + y if y in (0, ny - 1) else x * ny + ((y + 1) ^ 1) - 1
            far.append((x * ny + y, to))
    far = far[ny // 2 - 1 :] + far[: ny // 2 - 1]
    got = lax.ppermute(near_cells, "gy", near)
    there = lax.ppermute(far_cells, ("gx", "gy"), far)
    if far_first:
        at = lax.axis_index("gy")
        there = jnp.where((at > 0) & (at < ny - 1), there, jnp.zeros_like(there))
        there = lax.optimization_barrier(there)
    return got, there


def swap_x(near_cells, far_cells):
    nx, ny = lax.axis_size("gx"), lax.axis_size("gy")
    near = [(i, i ^ 1) for i in range(nx)]
    far = []
    for x in range(nx):
        for y in range(ny):
            to = x * ny + (y ^ 1) if x in (0, nx - 1) else (((x + 1) ^ 1) - 1) * ny + y
            far.append((x * ny + y, to))
    got = lax.ppermute(near_cells, "gx", near)
    return got, lax.ppermute(far_cells, ("gx", "gy"), far)


def local(
    volume,
    weight_entry,
    weight_down,
    weight_deep_first,
    weight_deep_second,
    weight_upward,
    weight_decoder,
):
    odd_x = lax.rem(lax.axis_index("gx"), 2)
    odd_y = lax.rem(lax.axis_index("gy"), 2)

    def column(array, at):
        return lax.dynamic_index_in_dim(array, at, axis=1, keepdims=False)

    def rows(array, at, count):
        return lax.dynamic_slice_in_dim(array, at, count, axis=0)

    def four_columns(pair, y_near, y_far, at):
        near, far = rows(y_near, at, 1), rows(y_far, at, 1)
        low = jnp.where(odd_y == 1, near, far)
        high = jnp.where(odd_y == 1, far, near)
        return jnp.concatenate([low, pair, high], axis=0)

    at_near, at_far = 7 * (1 - odd_x), 7 * odd_x
    sums = ((2, 8, 64, 128), F32)
    line = ((8, 64, 128), BF)
    own, near, far, edge_near, edge_far = call(
        prep_kernel,
        [((8, 2, 64, 128), BF), line, line, ((2, 64, 128), BF), ((2, 64, 128), BF)],
        [(None, None)],
        "prep",
        1_000_000,
        volume,
        remote=(0,),
    )
    y1, y2 = swap_y(near, far)
    total, entry = call(
        entry_own_kernel,
        [sums, ((3, 3, 384, 128), BF)],
        [((8, 64, 768), BF), ((3, 768, 256), BF), (None, None)],
        "entry_own",
        2_000_000_000,
        own,
        weight_entry.reshape(3, 3, 384, 128),
        remote=(1,),
    )
    x1, x2 = swap_x(
        four_columns(edge_near, y1, y2, at_near), four_columns(edge_far, y1, y2, at_far)
    )
    (total,) = call(
        entry_side_kernel,
        [sums],
        [((8, 64, 384), BF), ((8, 64, 384), BF)],
        "entry_side",
        1_000_000_000,
        y1,
        y2,
        entry,
        total,
    )
    encoded, coarse = call(
        entry_last_kernel,
        [((8, 2, 64, 128), BF), ((4, 32, 256), BF)],
        [((2, 64, 1536), BF), ((8, 2, 64, 128), F32), sums],
        "entry_last",
        1_000_000_000,
        x1,
        x2,
        entry,
        weight_down,
        total,
    )

    g1, g2 = swap_y(column(encoded, 1 - odd_y), column(encoded, odd_y))
    c1, c2 = swap_y(coarse, coarse)
    c_low = jnp.where(odd_y == 1, c1, c2)
    c_high = jnp.where(odd_y == 1, c2, c1)

    def coarse_edge(at):
        return jnp.stack([rows(c_low, at, 3), rows(coarse, at, 3), rows(c_high, at, 3)], axis=1)

    d1, d2 = swap_x(coarse_edge(1 - odd_x), coarse_edge(odd_x))
    (deep_one,) = call(
        first_kernel,
        [((8, 32, 256), BF)],
        [((10, 32, 2304), BF)],
        "first",
        1_000_000_000,
        coarse,
        c1,
        c2,
        d1,
        d2,
        weight_deep_first.reshape(3, 2304, 256),
    )
    f1, f2 = swap_y(deep_one, deep_one)
    skip, _ = lax.optimization_barrier(((encoded, g1, g2), deep_one))
    (total,) = call(
        decode_skip_kernel,
        [sums],
        [((8, 64, 768), BF), ((8, 64, 384), BF), ((8, 64, 384), BF), ((3, 768, 256), BF)],
        "decode_skip",
        2_000_000_000,
        *skip,
        weight_decoder,
    )
    edges = (
        four_columns(rows(encoded, at_near, 1)[0], g1, g2, at_near),
        four_columns(rows(encoded, at_far, 1)[0], g1, g2, at_far),
    )
    edges, total = lax.optimization_barrier((edges, total))
    e1, e2 = swap_x(*edges)
    (deep_two,) = call(
        second_kernel,
        [((6, 32, 256), BF)],
        [((8, 32, 2304), BF)],
        "second",
        700_000_000,
        deep_one,
        f1,
        f2,
        weight_deep_second.reshape(3, 2304, 256),
    )
    h1, h2 = swap_y(deep_two, deep_two, far_first=False)
    (total,) = call(
        decode_own_kernel,
        [sums],
        [
            ((10, 64, 768), BF),
            ((2, 64, 1536), BF),
            ((3, 768, 256), BF),
            ((10, 2, 64, 128), F32),
        ],
        "decode_own",
        2_000_000_000,
        deep_two,
        e1,
        e2,
        weight_upward,
        weight_decoder,
        total,
    )
    (total,) = call(
        decode_near_kernel,
        [sums],
        [((10, 64, 384), BF), ((10, 1, 64, 128), F32)],
        "decode_near",
        1_000_000_000,
        h1,
        weight_upward,
        weight_decoder,
        total,
    )
    (decoded,) = call(
        decode_last_kernel,
        [((8, 2, 64, 128), BF)],
        [((10, 64, 384), BF), ((10, 1, 64, 128), F32), sums],
        "decode_last",
        1_000_000_000,
        h2,
        weight_upward,
        weight_decoder,
        total,
    )
    return decoded


def solution(mesh):
    return jax.shard_map(
        local,
        mesh=mesh,
        in_specs=(P("gx", "gy", None, None), P(), P(), P(), P(), P(), P()),
        out_specs=P("gx", "gy", None, None),
        check_vma=False,
    )
```

```python
import jax
import jax.numpy as jnp
from jax import lax
from jax.experimental import pallas as pl
from jax.experimental.pallas import tpu as pltpu
from jax.sharding import PartitionSpec as P

BF = jnp.bfloat16
F32 = jnp.float32
LIMIT = 20 * 1024 * 1024


def leaky_unit(values):
    return jnp.where(values > 0, values, 0.1 * values)


def depth_sum(before, here, after, depth):
    at = lax.rem(lax.broadcasted_iota(jnp.int32, here.shape, 0), depth)
    count = here.shape[0]
    before = jnp.where(at == 0, 0.0, pltpu.roll(before, 1, axis=0))
    after = jnp.where(at == depth - 1, 0.0, pltpu.roll(after, count - 1, axis=0))
    return before + here + after


def three_rows(cells, first, rows):
    lanes = cells.shape[2]
    return jnp.concatenate(
        [
            cells[first + off : first + off + rows].reshape(rows * cells.shape[1], lanes)
            for off in range(3)
        ],
        axis=1,
    )


def own_sum(cells, part):
    left = three_rows(cells, 0, 8)
    products = []
    for d in range(3):
        blocks = []
        for off in range(3):
            blocks.append(jnp.concatenate([part(off, 1, d), part(off, 0, d)], axis=1))
            blocks.append(jnp.concatenate([part(off, 2, d), part(off, 1, d)], axis=1))
        products.append(
            jnp.dot(left, jnp.concatenate(blocks, axis=0), preferred_element_type=F32)
        )
    return depth_sum(*products, 64)


def taps_sum(left, blocks):
    right = jnp.concatenate([jnp.concatenate(parts, axis=0) for parts in blocks], axis=1)
    products = jnp.dot(left, right, preferred_element_type=F32)
    return depth_sum(*[products[:, d * 128 : d * 128 + 128] for d in range(3)], 64)


def side_sum(cells, part, side, first=0, rows=8):
    blocks = [[part(off, 2 * side, d) for off in range(3)] for d in range(3)]
    return taps_sum(three_rows(cells, first, rows), blocks).reshape(rows, 64, 128)


def add_rows(total, x_near, x_far, part):
    gx, nx = lax.axis_index("gx"), lax.axis_size("gx")
    odd_x = lax.rem(gx, 2)
    for cells, high, ok in ((x_near, 1 - odd_x, None), (x_far, odd_x, (gx > 0) & (gx < nx - 1))):
        for b in range(2):
            left = jnp.concatenate([cells[b + col] for col in range(3)], axis=1)
            blocks = [[part(2 * high, col, d) for col in range(3)] for d in range(3)]
            values = taps_sum(left, blocks)
            total[b, 7 * high] += values if ok is None else jnp.where(ok, values, 0.0)


def sides():
    odd = lax.rem(lax.axis_index("gy"), 2)
    return 1 - odd, odd


def clear_ends(cells):
    cells[0] = jnp.zeros_like(cells[0])
    cells[9] = jnp.zeros_like(cells[9])


def put_own(cells, own):
    clear_ends(cells)
    for b in range(2):
        cells[1:9, :, b * 128 : b * 128 + 128] = own[:, b]


def put_total(total, values):
    for b in range(2):
        total[b] = values[:, b * 128 : b * 128 + 128].reshape(8, 64, 128)


def prep_kernel(volume, own, near, far, edge_near, edge_far, sem):
    copy = pltpu.make_async_copy(volume, own, sem)
    copy.start()
    odd_x, odd_y = lax.rem(lax.axis_index("gx"), 2), lax.rem(lax.axis_index("gy"), 2)
    copy.wait()
    near[...] = own[:, 1 - odd_y]
    far[...] = own[:, odd_y]
    edge_near[...] = own[7 * (1 - odd_x)]
    edge_far[...] = own[7 * odd_x]


def entry_own_kernel(own, weight, total, cells):
    put_own(cells, own)
    put_total(total, own_sum(cells, lambda off, col, d: weight[off, col, d]))


def entry_side_kernel(y_near, y_far, weight, before, total, near, far):
    part = lambda off, col, d: weight[off, col, d]
    for cells, source, side in zip((near, far), (y_near, y_far), sides()):
        clear_ends(cells)
        cells[1:9] = source[...]
        total[side] = before[side] + side_sum(cells, part, side)


def entry_last_kernel(x_near, x_far, weight, down, before, encoded, coarse, fine, total):
    total[:, 0] = before[:, 0]
    total[:, 7] = before[:, 7]
    add_rows(total, x_near, x_far, lambda off, col, d: weight[off, col, d])

    def finish(row, source):
        for b in range(2):
            half = leaky_unit(source[b, row]).astype(BF)
            encoded[row, b] = half
            fine[row, b] = half.astype(F32)

    for row in range(1, 7):
        finish(row, before)
    finish(0, total)
    finish(7, total)
    small = jnp.zeros((128, 256), F32)
    for a in range(2):
        for d in range(2):
            cells = jnp.concatenate(
                [
                    jnp.concatenate(
                        [fine[2 * i + a, b, pl.ds(d, 32, stride=2), :] for b in range(2)], axis=1
                    )
                    for i in range(4)
                ],
                axis=0,
            ).astype(BF)
            small = small + jnp.dot(
                cells, down[a, :, d].reshape(256, 256), preferred_element_type=F32
            )
    coarse[...] = leaky_unit(small).astype(BF).reshape(4, 32, 256)


def deep_conv(rows, beyond, cells, weight, out):
    left = jnp.concatenate(
        [
            cells[plane, off : off + rows].reshape(rows * 32, 256)
            for off in range(3)
            for plane in range(3)
        ],
        axis=1,
    )
    products = [
        jnp.dot(left, weight[:, :, d].reshape(2304, 256), preferred_element_type=F32)
        for d in range(3)
    ]
    result = leaky_unit(depth_sum(*products, 32)).reshape(rows, 32, 256)
    gx, nx = lax.axis_index("gx"), lax.axis_size("gx")
    out[0:beyond] = jnp.where(gx > 0, result[0:beyond], 0.0).astype(BF)
    out[beyond : rows - beyond] = result[beyond : rows - beyond].astype(BF)
    out[rows - beyond :] = jnp.where(gx < nx - 1, result[rows - beyond :], 0.0).astype(BF)


def first_kernel(own, y_near, y_far, x_near, x_far, weight, out, cells):
    side_near, side_far = sides()
    gx, nx = lax.axis_index("gx"), lax.axis_size("gx")
    odd_x = lax.rem(gx, 2)
    cells[1, 3:7] = own[...]
    cells[2 * side_near, 3:7] = y_near[...]
    cells[2 * side_far, 3:7] = y_far[...]
    for plane in range(3):
        cells[plane, pl.ds(7 * (1 - odd_x), 3)] = x_near[:, plane]
        cells[plane, pl.ds(7 * odd_x, 3)] = jnp.where(
            (gx > 0) & (gx < nx - 1), x_far[:, plane].astype(F32), 0.0
        ).astype(BF)
    deep_conv(8, 2, cells, weight, out)


def deep_sum(planes, at, weight):
    left = jnp.concatenate([three_rows(p, 0, p.shape[0] - 2) for p in planes], axis=1)
    products = [
        jnp.dot(
            left,
            jnp.concatenate([weight[:, place, d].reshape(768, 256) for place in at], axis=0),
            preferred_element_type=F32,
        )
        for d in range(3)
    ]
    return depth_sum(*products, 32)


def second_own_kernel(own, y_near, weight, total):
    side, _ = sides()
    total[...] = deep_sum((own, y_near), (1, 2 * side), weight)


def second_far_kernel(y_far, weight, before, out):
    _, side = sides()
    gx, nx = lax.axis_index("gx"), lax.axis_size("gx")
    gy, ny = lax.axis_index("gy"), lax.axis_size("gy")
    far = jnp.where((gy > 0) & (gy < ny - 1), deep_sum((y_far,), (2 * side,), weight), 0.0)
    result = leaky_unit(before[...] + far).reshape(6, 32, 256)
    out[0] = jnp.where(gx > 0, result[0], 0.0).astype(BF)
    out[1:5] = result[1:5].astype(BF)
    out[5] = jnp.where(gx < nx - 1, result[5], 0.0).astype(BF)


def half_weights(weight, half):
    return lambda off, col, d: weight[off, col, d, half * 128 : half * 128 + 128]


def lift(cells, up, b, upward, col):
    for a in range(2):
        for d in range(2):
            part = leaky_unit(jnp.dot(cells, up[a, b, d], preferred_element_type=F32))
            part = part.reshape(6, 32, 128)
            for i in range(6):
                row = 2 * i + a - 1
                if 0 <= row < 10:
                    upward[row, col, pl.ds(d, 32, stride=2), :] = part[i]


def decode_skip_kernel(encoded, y_near, y_far, weight, total, own, near, far):
    part = half_weights(weight, 1)
    put_own(own, encoded)
    put_total(total, own_sum(own, part))
    for cells, source, side in zip((near, far), (y_near, y_far), sides()):
        clear_ends(cells)
        cells[1:9] = source[...]
        total[side] += side_sum(cells, part, side)


def decode_own_kernel(own, x_near, x_far, up, weight, before, total, cells, upward):
    lift(own[...].reshape(192, 256), up, 0, upward, 0)
    lift(own[...].reshape(192, 256), up, 1, upward, 1)
    for b in range(2):
        cells[:, :, b * 128 : b * 128 + 128] = upward[:, b].astype(BF)
    values = own_sum(cells, half_weights(weight, 0))
    for b in range(2):
        total[b] = before[b] + values[:, b * 128 : b * 128 + 128].reshape(8, 64, 128)
    add_rows(total, x_near, x_far, half_weights(weight, 1))


def decode_near_kernel(y_near, up, weight, before, decoded, cells, upward, column, sem):
    side, _ = sides()
    lift(y_near[...].reshape(192, 256), up, 1 - side, upward, 0)
    cells[...] = upward[:, 0].astype(BF)
    values = before[side] + side_sum(cells, half_weights(weight, 0), side)
    column[...] = leaky_unit(values).astype(BF)
    copy = pltpu.make_async_copy(column, decoded.at[:, side], sem)
    copy.start()
    copy.wait()


def decode_last_kernel(y_far, up, weight, before, _, decoded, cells, upward, column, sems):
    _, side = sides()
    gy, ny = lax.axis_index("gy"), lax.axis_size("gy")
    lift(y_far[...].reshape(192, 256), up, 1 - side, upward, 0)
    cells[...] = jnp.where((gy > 0) & (gy < ny - 1), upward[:, 0], 0.0).astype(BF)
    copies = []
    for half in range(2):
        rows = slice(4 * half, 4 * half + 4)
        values = before[side, rows] + side_sum(cells, half_weights(weight, 0), side, 4 * half, 4)
        column[rows] = leaky_unit(values).astype(BF)
        copies.append(
            pltpu.make_async_copy(column.at[rows], decoded.at[rows, side], sems.at[half])
        )
        copies[-1].start()
    for copy in copies:
        copy.wait()


def call(kernel, outs, scratch, name, flops, *operands, remote=(), hbm_out=False, aliases=()):
    vmem = pl.BlockSpec(memory_space=pltpu.VMEM)
    hbm = pl.BlockSpec(memory_space=pltpu.HBM)
    return pl.pallas_call(
        kernel,
        out_shape=[jax.ShapeDtypeStruct(shape, dtype) for shape, dtype in outs],
        in_specs=[hbm if i in remote else vmem for i in range(len(operands))],
        out_specs=[hbm if hbm_out else vmem] * len(outs),
        scratch_shapes=[
            pltpu.SemaphoreType.DMA(shape) if dtype is None else pltpu.VMEM(shape, dtype)
            for shape, dtype in scratch
        ],
        compiler_params=pltpu.CompilerParams(vmem_limit_bytes=LIMIT),
        cost_estimate=pl.CostEstimate(flops=flops, bytes_accessed=1 << 20, transcendentals=0),
        input_output_aliases=dict(aliases),
        name=name,
    )(*operands)


def swap_y(near_cells, far_cells, far_first=True):
    nx, ny = lax.axis_size("gx"), lax.axis_size("gy")
    near = [(i, i ^ 1) for i in range(ny)]
    far = []
    for x in range(nx):
        for y in range(ny):
            to = (x ^ 1) * ny + y if y in (0, ny - 1) else x * ny + ((y + 1) ^ 1) - 1
            far.append((x * ny + y, to))
    far = far[ny // 2 - 1 :] + far[: ny // 2 - 1]
    got = lax.ppermute(near_cells, "gy", near)
    there = lax.ppermute(far_cells, ("gx", "gy"), far)
    if far_first:
        at = lax.axis_index("gy")
        there = jnp.where((at > 0) & (at < ny - 1), there, jnp.zeros_like(there))
        there = lax.optimization_barrier(there)
    return got, there


def swap_x(near_cells, far_cells):
    nx, ny = lax.axis_size("gx"), lax.axis_size("gy")
    near = [(i, i ^ 1) for i in range(nx)]
    far = []
    for x in range(nx):
        for y in range(ny):
            idle = y ^ 4 if ny >= 8 else y ^ 1
            to = x * ny + idle if x in (0, nx - 1) else (((x + 1) ^ 1) - 1) * ny + y
            far.append((x * ny + y, to))
    got = lax.ppermute(near_cells, "gx", near)
    return got, lax.ppermute(far_cells, ("gx", "gy"), far)


def local(
    volume,
    weight_entry,
    weight_down,
    weight_deep_first,
    weight_deep_second,
    weight_upward,
    weight_decoder,
):
    odd_x = lax.rem(lax.axis_index("gx"), 2)
    odd_y = lax.rem(lax.axis_index("gy"), 2)

    def column(array, at):
        return lax.dynamic_index_in_dim(array, at, axis=1, keepdims=False)

    def rows(array, at, count):
        return lax.dynamic_slice_in_dim(array, at, count, axis=0)

    def four_columns(pair, y_near, y_far, at):
        near, far = rows(y_near, at, 1), rows(y_far, at, 1)
        low = jnp.where(odd_y == 1, near, far)
        high = jnp.where(odd_y == 1, far, near)
        return jnp.concatenate([low, pair, high], axis=0)

    at_near, at_far = 7 * (1 - odd_x), 7 * odd_x
    sums = ((2, 8, 64, 128), F32)
    line = ((8, 64, 128), BF)
    tall = ((10, 64, 128), BF)
    wide = ((10, 64, 256), BF)
    own, near, far, edge_near, edge_far = call(
        prep_kernel,
        [((8, 2, 64, 128), BF), line, line, ((2, 64, 128), BF), ((2, 64, 128), BF)],
        [((), None)],
        "prep",
        1_000_000,
        volume,
        remote=(0,),
    )
    y1, y2 = swap_y(near, far)
    (total,) = call(
        entry_own_kernel, [sums], [wide], "entry_own", 2_000_000_000, own, weight_entry
    )
    x1, x2 = swap_x(
        four_columns(edge_near, y1, y2, at_near), four_columns(edge_far, y1, y2, at_far)
    )
    (total,) = call(
        entry_side_kernel,
        [sums],
        [tall, tall],
        "entry_side",
        1_000_000_000,
        y1,
        y2,
        weight_entry,
        total,
    )
    encoded, coarse = call(
        entry_last_kernel,
        [((8, 2, 64, 128), BF), ((4, 32, 256), BF)],
        [((8, 2, 64, 128), F32), sums],
        "entry_last",
        1_000_000_000,
        x1,
        x2,
        weight_entry,
        weight_down,
        total,
    )

    g1, g2 = swap_y(column(encoded, 1 - odd_y), column(encoded, odd_y))
    c1, c2 = swap_y(coarse, coarse)
    c_low = jnp.where(odd_y == 1, c1, c2)
    c_high = jnp.where(odd_y == 1, c2, c1)

    def coarse_edge(at):
        return jnp.stack([rows(c_low, at, 3), rows(coarse, at, 3), rows(c_high, at, 3)], axis=1)

    d1, d2 = swap_x(coarse_edge(1 - odd_x), coarse_edge(odd_x))
    (deep_one,) = call(
        first_kernel,
        [((8, 32, 256), BF)],
        [((3, 10, 32, 256), BF)],
        "first",
        1_000_000_000,
        coarse,
        c1,
        c2,
        d1,
        d2,
        weight_deep_first,
    )
    f1, f2 = swap_y(deep_one, deep_one, far_first=False)
    skip, _ = lax.optimization_barrier(((encoded, g1, g2), deep_one))
    (total,) = call(
        decode_skip_kernel,
        [sums],
        [wide, tall, tall],
        "decode_skip",
        2_000_000_000,
        *skip,
        weight_decoder,
    )
    edges = (
        four_columns(rows(encoded, at_near, 1)[0], g1, g2, at_near),
        four_columns(rows(encoded, at_far, 1)[0], g1, g2, at_far),
    )
    edges, total = lax.optimization_barrier((edges, total))
    e1, e2 = swap_x(*edges)
    (part,) = call(
        second_own_kernel,
        [((192, 256), F32)],
        [],
        "second_own",
        700_000_000,
        deep_one,
        f1,
        weight_deep_second,
    )
    (deep_two,) = call(
        second_far_kernel,
        [((6, 32, 256), BF)],
        [],
        "second_far",
        500_000_000,
        f2,
        weight_deep_second,
        part,
    )
    h1, h2 = swap_y(deep_two, deep_two, far_first=False)
    upward = ((10, 1, 64, 128), F32)
    (total,) = call(
        decode_own_kernel,
        [sums],
        [wide, ((10, 2, 64, 128), F32)],
        "decode_own",
        2_000_000_000,
        deep_two,
        e1,
        e2,
        weight_upward,
        weight_decoder,
        total,
    )
    (decoded,) = call(
        decode_near_kernel,
        [((8, 2, 64, 128), BF)],
        [tall, upward, line, ((), None)],
        "decode_near",
        1_000_000_000,
        h1,
        weight_upward,
        weight_decoder,
        total,
        hbm_out=True,
    )
    (decoded,) = call(
        decode_last_kernel,
        [((8, 2, 64, 128), BF)],
        [tall, upward, line, ((2,), None)],
        "decode_last",
        1_000_000_000,
        h2,
        weight_upward,
        weight_decoder,
        total,
        decoded,
        remote=(4,),
        hbm_out=True,
        aliases=((4, 0),),
    )
    return decoded


def solution(mesh):
    return jax.shard_map(
        local,
        mesh=mesh,
        in_specs=(P("gx", "gy", None, None), P(), P(), P(), P(), P(), P()),
        out_specs=P("gx", "gy", None, None),
        check_vma=False,
    )
```

```python
import jax
import jax.numpy as jnp
from jax import lax
from jax.experimental import pallas as pl
from jax.experimental.pallas import tpu as pltpu
from jax.sharding import PartitionSpec as P

BF = jnp.bfloat16
F32 = jnp.float32
LIMIT = 20 * 1024 * 1024


def leaky_unit(values):
    return jnp.where(values > 0, values, 0.1 * values)


def depth_sum(before, here, after, depth):
    at = lax.rem(lax.broadcasted_iota(jnp.int32, here.shape, 0), depth)
    count = here.shape[0]
    before = jnp.where(at == 0, 0.0, pltpu.roll(before, 1, axis=0))
    after = jnp.where(at == depth - 1, 0.0, pltpu.roll(after, count - 1, axis=0))
    return before + here + after


def three_rows(cells, first, rows):
    lanes = cells.shape[2]
    return jnp.concatenate(
        [
            cells[first + off : first + off + rows].reshape(rows * cells.shape[1], lanes)
            for off in range(3)
        ],
        axis=1,
    )


def own_sum(cells, part):
    left = three_rows(cells, 0, 8)
    products = []
    for d in range(3):
        blocks = []
        for off in range(3):
            blocks.append(jnp.concatenate([part(off, 1, d), part(off, 0, d)], axis=1))
            blocks.append(jnp.concatenate([part(off, 2, d), part(off, 1, d)], axis=1))
        products.append(
            jnp.dot(left, jnp.concatenate(blocks, axis=0), preferred_element_type=F32)
        )
    return depth_sum(*products, 64)


def taps_sum(left, blocks):
    right = jnp.concatenate([jnp.concatenate(parts, axis=0) for parts in blocks], axis=1)
    products = jnp.dot(left, right, preferred_element_type=F32)
    return depth_sum(*[products[:, d * 128 : d * 128 + 128] for d in range(3)], 64)


def side_sum(cells, part, side, first=0, rows=8):
    blocks = [[part(off, 2 * side, d) for off in range(3)] for d in range(3)]
    return taps_sum(three_rows(cells, first, rows), blocks).reshape(rows, 64, 128)


def add_rows(total, x_near, x_far, part):
    gx, nx = lax.axis_index("gx"), lax.axis_size("gx")
    odd_x = lax.rem(gx, 2)
    for cells, high, ok in ((x_near, 1 - odd_x, None), (x_far, odd_x, (gx > 0) & (gx < nx - 1))):
        for b in range(2):
            left = jnp.concatenate([cells[b + col] for col in range(3)], axis=1)
            blocks = [[part(2 * high, col, d) for col in range(3)] for d in range(3)]
            values = taps_sum(left, blocks)
            total[b, 7 * high] += values if ok is None else jnp.where(ok, values, 0.0)


def sides():
    odd = lax.rem(lax.axis_index("gy"), 2)
    return 1 - odd, odd


def clear_ends(cells):
    cells[0] = jnp.zeros_like(cells[0])
    cells[9] = jnp.zeros_like(cells[9])


def put_own(cells, own):
    clear_ends(cells)
    for b in range(2):
        cells[1:9, :, b * 128 : b * 128 + 128] = own[:, b]


def put_total(total, values):
    for b in range(2):
        total[b] = values[:, b * 128 : b * 128 + 128].reshape(8, 64, 128)


def prep_kernel(volume, own, near, far, edge_near, edge_far, sem):
    copy = pltpu.make_async_copy(volume, own, sem)
    copy.start()
    odd_x, odd_y = lax.rem(lax.axis_index("gx"), 2), lax.rem(lax.axis_index("gy"), 2)
    copy.wait()
    near[...] = own[:, 1 - odd_y]
    far[...] = own[:, odd_y]
    edge_near[...] = own[7 * (1 - odd_x)]
    edge_far[...] = own[7 * odd_x]


def entry_own_kernel(own, weight, total, cells):
    put_own(cells, own)
    put_total(total, own_sum(cells, lambda off, col, d: weight[off, col, d]))


def entry_side_kernel(y_near, y_far, weight, before, total, near, far):
    part = lambda off, col, d: weight[off, col, d]
    for cells, source, side in zip((near, far), (y_near, y_far), sides()):
        clear_ends(cells)
        cells[1:9] = source[...]
        total[side] = before[side] + side_sum(cells, part, side)


def entry_last_kernel(x_near, x_far, weight, down, before, encoded, coarse, fine, total):
    total[:, 0] = before[:, 0]
    total[:, 7] = before[:, 7]
    add_rows(total, x_near, x_far, lambda off, col, d: weight[off, col, d])

    def finish(row, source):
        for b in range(2):
            half = leaky_unit(source[b, row]).astype(BF)
            encoded[row, b] = half
            fine[row, b] = half.astype(F32)

    for row in range(1, 7):
        finish(row, before)
    finish(0, total)
    finish(7, total)
    small = jnp.zeros((128, 256), F32)
    for a in range(2):
        for d in range(2):
            cells = jnp.concatenate(
                [
                    jnp.concatenate(
                        [fine[2 * i + a, b, pl.ds(d, 32, stride=2), :] for b in range(2)], axis=1
                    )
                    for i in range(4)
                ],
                axis=0,
            ).astype(BF)
            small = small + jnp.dot(
                cells, down[a, :, d].reshape(256, 256), preferred_element_type=F32
            )
    coarse[...] = leaky_unit(small).astype(BF).reshape(4, 32, 256)


def masked_rows(result, beyond, out):
    rows = out.shape[0]
    gx, nx = lax.axis_index("gx"), lax.axis_size("gx")
    out[0:beyond] = jnp.where(gx > 0, result[0:beyond], 0.0).astype(BF)
    out[beyond : rows - beyond] = result[beyond : rows - beyond].astype(BF)
    out[rows - beyond :] = jnp.where(gx < nx - 1, result[rows - beyond :], 0.0).astype(BF)


def rows_sum(rows, weight, off):
    left = jnp.concatenate([jnp.concatenate(planes, axis=1) for planes in rows], axis=0)
    products = [
        jnp.dot(left, weight[off, :, d].reshape(768, 256), preferred_element_type=F32)
        for d in range(3)
    ]
    return depth_sum(*products, 32).reshape(len(rows), 32, 256)


def first_own_kernel(own, y_near, y_far, weight, total, cells):
    near, far = sides()
    cells[1] = own[...]
    cells[2 * near] = y_near[...]
    cells[2 * far] = y_far[...]
    rows = [[cells[plane, row] for plane in range(3)] for row in range(4)]
    total[...] = jnp.zeros_like(total)
    for off in range(3):
        total[3 - off : 7 - off] += rows_sum(rows, weight, off)


def first_last_kernel(x_near, x_far, weight, before, out, cells, total):
    gx, nx = lax.axis_index("gx"), lax.axis_size("gx")
    odd_x = lax.rem(gx, 2)
    cells[1 - odd_x] = x_near[...]
    cells[odd_x] = jnp.where((gx > 0) & (gx < nx - 1), x_far[...].astype(F32), 0.0).astype(BF)
    rows = [[cells[k // 3, k % 3, plane] for plane in range(3)] for k in range(6)]
    total[...] = before[...]
    for off in range(3):
        part = rows_sum(rows[off : off + 4], weight, off)
        below = 3 - off
        total[0:below] += part[0:below]
        total[7 - off : 8] += part[below:]
    masked_rows(leaky_unit(total[...]), 2, out)


def deep_sum(planes, at, weight):
    left = jnp.concatenate([three_rows(p, 0, p.shape[0] - 2) for p in planes], axis=1)
    products = [
        jnp.dot(
            left,
            jnp.concatenate([weight[:, place, d].reshape(768, 256) for place in at], axis=0),
            preferred_element_type=F32,
        )
        for d in range(3)
    ]
    return depth_sum(*products, 32)


def second_own_kernel(own, y_near, weight, total):
    side, _ = sides()
    total[...] = deep_sum((own, y_near), (1, 2 * side), weight)


def second_far_kernel(y_far, weight, before, out):
    _, side = sides()
    gy, ny = lax.axis_index("gy"), lax.axis_size("gy")
    far = jnp.where((gy > 0) & (gy < ny - 1), deep_sum((y_far,), (2 * side,), weight), 0.0)
    masked_rows(leaky_unit(before[...] + far).reshape(6, 32, 256), 1, out)


def half_weights(weight, half):
    return lambda off, col, d: weight[off, col, d, half * 128 : half * 128 + 128]


def lift(cells, up, b, upward, col):
    for a in range(2):
        for d in range(2):
            part = leaky_unit(jnp.dot(cells, up[a, b, d], preferred_element_type=F32))
            part = part.reshape(6, 32, 128)
            for i in range(6):
                row = 2 * i + a - 1
                if 0 <= row < 10:
                    upward[row, col, pl.ds(d, 32, stride=2), :] = part[i]


def decode_skip_kernel(encoded, y_near, y_far, weight, total, own, near, far):
    part = half_weights(weight, 1)
    put_own(own, encoded)
    put_total(total, own_sum(own, part))
    for cells, source, side in zip((near, far), (y_near, y_far), sides()):
        clear_ends(cells)
        cells[1:9] = source[...]
        total[side] += side_sum(cells, part, side)


def decode_own_kernel(own, x_near, x_far, up, weight, before, total, cells, upward):
    lift(own[...].reshape(192, 256), up, 0, upward, 0)
    lift(own[...].reshape(192, 256), up, 1, upward, 1)
    for b in range(2):
        cells[:, :, b * 128 : b * 128 + 128] = upward[:, b].astype(BF)
    values = own_sum(cells, half_weights(weight, 0))
    for b in range(2):
        total[b] = before[b] + values[:, b * 128 : b * 128 + 128].reshape(8, 64, 128)
    add_rows(total, x_near, x_far, half_weights(weight, 1))


def decode_near_kernel(y_near, up, weight, before, decoded, cells, upward, column, sem):
    side, _ = sides()
    lift(y_near[...].reshape(192, 256), up, 1 - side, upward, 0)
    cells[...] = upward[:, 0].astype(BF)
    values = before[side] + side_sum(cells, half_weights(weight, 0), side)
    column[...] = leaky_unit(values).astype(BF)
    copy = pltpu.make_async_copy(column, decoded.at[:, side], sem)
    copy.start()
    copy.wait()


def decode_last_kernel(y_far, up, weight, before, _, decoded, cells, upward, column, sems):
    _, side = sides()
    gy, ny = lax.axis_index("gy"), lax.axis_size("gy")
    lift(y_far[...].reshape(192, 256), up, 1 - side, upward, 0)
    cells[...] = jnp.where((gy > 0) & (gy < ny - 1), upward[:, 0], 0.0).astype(BF)
    copies = []
    for half in range(2):
        rows = slice(4 * half, 4 * half + 4)
        values = before[side, rows] + side_sum(cells, half_weights(weight, 0), side, 4 * half, 4)
        column[rows] = leaky_unit(values).astype(BF)
        copies.append(
            pltpu.make_async_copy(column.at[rows], decoded.at[rows, side], sems.at[half])
        )
        copies[-1].start()
    for copy in copies:
        copy.wait()


def call(kernel, outs, scratch, name, flops, *operands, remote=(), hbm_out=False, aliases=()):
    vmem = pl.BlockSpec(memory_space=pltpu.VMEM)
    hbm = pl.BlockSpec(memory_space=pltpu.HBM)
    return pl.pallas_call(
        kernel,
        out_shape=[jax.ShapeDtypeStruct(shape, dtype) for shape, dtype in outs],
        in_specs=[hbm if i in remote else vmem for i in range(len(operands))],
        out_specs=[hbm if hbm_out else vmem] * len(outs),
        scratch_shapes=[
            pltpu.SemaphoreType.DMA(shape) if dtype is None else pltpu.VMEM(shape, dtype)
            for shape, dtype in scratch
        ],
        compiler_params=pltpu.CompilerParams(vmem_limit_bytes=LIMIT),
        cost_estimate=pl.CostEstimate(flops=flops, bytes_accessed=1 << 20, transcendentals=0),
        input_output_aliases=dict(aliases),
        name=name,
    )(*operands)


def swap_y(near_cells, far_cells, far_first=True):
    nx, ny = lax.axis_size("gx"), lax.axis_size("gy")
    near = [(i, i ^ 1) for i in range(ny)]
    far = []
    for x in range(nx):
        for y in range(ny):
            to = (x ^ 1) * ny + y if y in (0, ny - 1) else x * ny + ((y + 1) ^ 1) - 1
            far.append((x * ny + y, to))
    far = far[ny // 2 - 1 :] + far[: ny // 2 - 1]
    got = lax.ppermute(near_cells, "gy", near)
    there = lax.ppermute(far_cells, ("gx", "gy"), far)
    if far_first:
        at = lax.axis_index("gy")
        there = jnp.where((at > 0) & (at < ny - 1), there, jnp.zeros_like(there))
        there = lax.optimization_barrier(there)
    return got, there


def swap_x(near_cells, far_cells):
    nx, ny = lax.axis_size("gx"), lax.axis_size("gy")
    near = [(i, i ^ 1) for i in range(nx)]
    far = []
    for x in range(nx):
        for y in range(ny):
            idle = y ^ 4 if ny >= 8 else y ^ 1
            to = x * ny + idle if x in (0, nx - 1) else (((x + 1) ^ 1) - 1) * ny + y
            far.append((x * ny + y, to))
    got = lax.ppermute(near_cells, "gx", near)
    return got, lax.ppermute(far_cells, ("gx", "gy"), far)


def local(
    volume,
    weight_entry,
    weight_down,
    weight_deep_first,
    weight_deep_second,
    weight_upward,
    weight_decoder,
):
    odd_x = lax.rem(lax.axis_index("gx"), 2)
    odd_y = lax.rem(lax.axis_index("gy"), 2)

    def column(array, at):
        return lax.dynamic_index_in_dim(array, at, axis=1, keepdims=False)

    def rows(array, at, count):
        return lax.dynamic_slice_in_dim(array, at, count, axis=0)

    def four_columns(pair, y_near, y_far, at):
        near, far = rows(y_near, at, 1), rows(y_far, at, 1)
        low = jnp.where(odd_y == 1, near, far)
        high = jnp.where(odd_y == 1, far, near)
        return jnp.concatenate([low, pair, high], axis=0)

    at_near, at_far = 7 * (1 - odd_x), 7 * odd_x
    sums = ((2, 8, 64, 128), F32)
    line = ((8, 64, 128), BF)
    tall = ((10, 64, 128), BF)
    wide = ((10, 64, 256), BF)
    own, near, far, edge_near, edge_far = call(
        prep_kernel,
        [((8, 2, 64, 128), BF), line, line, ((2, 64, 128), BF), ((2, 64, 128), BF)],
        [((), None)],
        "prep",
        1_000_000,
        volume,
        remote=(0,),
    )
    y1, y2 = swap_y(near, far)
    (total,) = call(
        entry_own_kernel, [sums], [wide], "entry_own", 2_000_000_000, own, weight_entry
    )
    x1, x2 = swap_x(
        four_columns(edge_near, y1, y2, at_near), four_columns(edge_far, y1, y2, at_far)
    )
    (total,) = call(
        entry_side_kernel,
        [sums],
        [tall, tall],
        "entry_side",
        1_000_000_000,
        y1,
        y2,
        weight_entry,
        total,
    )
    encoded, coarse = call(
        entry_last_kernel,
        [((8, 2, 64, 128), BF), ((4, 32, 256), BF)],
        [((8, 2, 64, 128), F32), sums],
        "entry_last",
        1_000_000_000,
        x1,
        x2,
        weight_entry,
        weight_down,
        total,
    )

    g1, g2 = swap_y(column(encoded, 1 - odd_y), column(encoded, odd_y))
    c1, c2 = swap_y(coarse, coarse)
    c_low = jnp.where(odd_y == 1, c1, c2)
    c_high = jnp.where(odd_y == 1, c2, c1)

    def coarse_edge(at):
        return jnp.stack([rows(c_low, at, 3), rows(coarse, at, 3), rows(c_high, at, 3)], axis=1)

    d1, d2 = swap_x(coarse_edge(1 - odd_x), coarse_edge(odd_x))
    (part,) = call(
        first_own_kernel,
        [((8, 32, 256), F32)],
        [((3, 4, 32, 256), BF)],
        "first_own",
        700_000_000,
        coarse,
        c1,
        c2,
        weight_deep_first,
    )
    (deep_one,) = call(
        first_last_kernel,
        [((8, 32, 256), BF)],
        [((2, 3, 3, 32, 256), BF), ((8, 32, 256), F32)],
        "first_last",
        1_000_000_000,
        d1,
        d2,
        weight_deep_first,
        part,
    )
    f1, f2 = swap_y(deep_one, deep_one, far_first=False)
    skip, _ = lax.optimization_barrier(((encoded, g1, g2), deep_one))
    (total,) = call(
        decode_skip_kernel,
        [sums],
        [wide, tall, tall],
        "decode_skip",
        2_000_000_000,
        *skip,
        weight_decoder,
    )
    edges = (
        four_columns(rows(encoded, at_near, 1)[0], g1, g2, at_near),
        four_columns(rows(encoded, at_far, 1)[0], g1, g2, at_far),
    )
    edges, total = lax.optimization_barrier((edges, total))
    e1, e2 = swap_x(*edges)
    (part,) = call(
        second_own_kernel,
        [((192, 256), F32)],
        [],
        "second_own",
        700_000_000,
        deep_one,
        f1,
        weight_deep_second,
    )
    (deep_two,) = call(
        second_far_kernel,
        [((6, 32, 256), BF)],
        [],
        "second_far",
        500_000_000,
        f2,
        weight_deep_second,
        part,
    )
    h1, h2 = swap_y(deep_two, deep_two, far_first=False)
    upward = ((10, 1, 64, 128), F32)
    (total,) = call(
        decode_own_kernel,
        [sums],
        [wide, ((10, 2, 64, 128), F32)],
        "decode_own",
        2_000_000_000,
        deep_two,
        e1,
        e2,
        weight_upward,
        weight_decoder,
        total,
    )
    (decoded,) = call(
        decode_near_kernel,
        [((8, 2, 64, 128), BF)],
        [tall, upward, line, ((), None)],
        "decode_near",
        1_000_000_000,
        h1,
        weight_upward,
        weight_decoder,
        total,
        hbm_out=True,
    )
    (decoded,) = call(
        decode_last_kernel,
        [((8, 2, 64, 128), BF)],
        [tall, upward, line, ((2,), None)],
        "decode_last",
        1_000_000_000,
        h2,
        weight_upward,
        weight_decoder,
        total,
        decoded,
        remote=(4,),
        hbm_out=True,
        aliases=((4, 0),),
    )
    return decoded


def solution(mesh):
    return jax.shard_map(
        local,
        mesh=mesh,
        in_specs=(P("gx", "gy", None, None), P(), P(), P(), P(), P(), P()),
        out_specs=P("gx", "gy", None, None),
        check_vma=False,
    )
```

```python
import jax
import jax.numpy as jnp
from jax import lax
from jax.experimental import pallas as pl
from jax.experimental.pallas import tpu as pltpu
from jax.sharding import PartitionSpec as P

BF = jnp.bfloat16
F32 = jnp.float32
LIMIT = 20 * 1024 * 1024


def leaky_unit(values):
    return jnp.where(values > 0, values, 0.1 * values)


def depth_sum(before, here, after, depth):
    at = lax.rem(lax.broadcasted_iota(jnp.int32, here.shape, 0), depth)
    count = here.shape[0]
    before = jnp.where(at == 0, 0.0, pltpu.roll(before, 1, axis=0))
    after = jnp.where(at == depth - 1, 0.0, pltpu.roll(after, count - 1, axis=0))
    return before + here + after


def three_rows(cells, first, rows):
    lanes = cells.shape[2]
    return jnp.concatenate(
        [
            cells[first + off : first + off + rows].reshape(rows * cells.shape[1], lanes)
            for off in range(3)
        ],
        axis=1,
    )


def own_sum(cells, part):
    left = three_rows(cells, 0, 8)
    products = []
    for d in range(3):
        blocks = []
        for off in range(3):
            blocks.append(jnp.concatenate([part(off, 1, d), part(off, 0, d)], axis=1))
            blocks.append(jnp.concatenate([part(off, 2, d), part(off, 1, d)], axis=1))
        products.append(
            jnp.dot(left, jnp.concatenate(blocks, axis=0), preferred_element_type=F32)
        )
    return depth_sum(*products, 64)


def taps_sum(left, blocks):
    right = jnp.concatenate([jnp.concatenate(parts, axis=0) for parts in blocks], axis=1)
    products = jnp.dot(left, right, preferred_element_type=F32)
    return depth_sum(*[products[:, d * 128 : d * 128 + 128] for d in range(3)], 64)


def side_sum(cells, part, side, first=0, rows=8):
    blocks = [[part(off, 2 * side, d) for off in range(3)] for d in range(3)]
    return taps_sum(three_rows(cells, first, rows), blocks).reshape(rows, 64, 128)


def add_rows(total, x_near, x_far, part):
    gx, nx = lax.axis_index("gx"), lax.axis_size("gx")
    odd_x = lax.rem(gx, 2)
    for cells, high, ok in ((x_near, 1 - odd_x, None), (x_far, odd_x, (gx > 0) & (gx < nx - 1))):
        left = jnp.concatenate(
            [jnp.concatenate([cells[b + col] for col in range(3)], axis=1) for b in range(2)],
            axis=0,
        )
        blocks = [[part(2 * high, col, d) for col in range(3)] for d in range(3)]
        values = taps_sum(left, blocks)
        if ok is not None:
            values = jnp.where(ok, values, 0.0)
        for b in range(2):
            total[b, 7 * high] += values[b * 64 : b * 64 + 64]


def sides():
    odd = lax.rem(lax.axis_index("gy"), 2)
    return 1 - odd, odd


def clear_ends(cells):
    cells[0] = jnp.zeros_like(cells[0])
    cells[9] = jnp.zeros_like(cells[9])


def put_own(cells, own):
    clear_ends(cells)
    for b in range(2):
        cells[1:9, :, b * 128 : b * 128 + 128] = own[:, b]


def put_total(total, values):
    for b in range(2):
        total[b] = values[:, b * 128 : b * 128 + 128].reshape(8, 64, 128)


def prep_kernel(volume, own, near, far, edge_near, edge_far, sem):
    copy = pltpu.make_async_copy(volume, own, sem)
    copy.start()
    odd_x, odd_y = lax.rem(lax.axis_index("gx"), 2), lax.rem(lax.axis_index("gy"), 2)
    copy.wait()
    near[...] = own[:, 1 - odd_y]
    far[...] = own[:, odd_y]
    edge_near[...] = own[7 * (1 - odd_x)]
    edge_far[...] = own[7 * odd_x]


def entry_own_kernel(own, weight, total, cells):
    put_own(cells, own)
    put_total(total, own_sum(cells, lambda off, col, d: weight[off, col, d]))


def entry_side_kernel(y_near, y_far, weight, before, total, near, far):
    part = lambda off, col, d: weight[off, col, d]
    for cells, source, side in zip((near, far), (y_near, y_far), sides()):
        clear_ends(cells)
        cells[1:9] = source[...]
        total[side] = before[side] + side_sum(cells, part, side)


def entry_last_kernel(x_near, x_far, weight, down, before, encoded, coarse, fine, total):
    total[:, 0] = before[:, 0]
    total[:, 7] = before[:, 7]
    add_rows(total, x_near, x_far, lambda off, col, d: weight[off, col, d])

    def finish(row, source):
        for b in range(2):
            half = leaky_unit(source[b, row]).astype(BF)
            encoded[row, b] = half
            fine[row, b] = half.astype(F32)

    for row in range(1, 7):
        finish(row, before)
    finish(0, total)
    finish(7, total)
    small = jnp.zeros((128, 256), F32)
    for a in range(2):
        for d in range(2):
            cells = jnp.concatenate(
                [
                    jnp.concatenate(
                        [fine[2 * i + a, b, pl.ds(d, 32, stride=2), :] for b in range(2)], axis=1
                    )
                    for i in range(4)
                ],
                axis=0,
            ).astype(BF)
            small = small + jnp.dot(
                cells, down[a, :, d].reshape(256, 256), preferred_element_type=F32
            )
    coarse[...] = leaky_unit(small).astype(BF).reshape(4, 32, 256)


def masked_rows(result, beyond, out):
    rows = out.shape[0]
    gx, nx = lax.axis_index("gx"), lax.axis_size("gx")
    out[0:beyond] = jnp.where(gx > 0, result[0:beyond], 0.0).astype(BF)
    out[beyond : rows - beyond] = result[beyond : rows - beyond].astype(BF)
    out[rows - beyond :] = jnp.where(gx < nx - 1, result[rows - beyond :], 0.0).astype(BF)


def rows_sum(rows, weight, off):
    left = jnp.concatenate([jnp.concatenate(planes, axis=1) for planes in rows], axis=0)
    right = jnp.concatenate([weight[off, :, d].reshape(768, 256) for d in range(3)], axis=1)
    products = jnp.dot(left, right, preferred_element_type=F32)
    products = [products[:, d * 256 : d * 256 + 256] for d in range(3)]
    return depth_sum(*products, 32).reshape(len(rows), 32, 256)


def first_own_kernel(own, y_near, y_far, weight, total, cells):
    near, far = sides()
    cells[1] = own[...]
    cells[2 * near] = y_near[...]
    cells[2 * far] = y_far[...]
    rows = [[cells[plane, row] for plane in range(3)] for row in range(4)]
    total[...] = jnp.zeros_like(total)
    for off in range(3):
        total[3 - off : 7 - off] += rows_sum(rows, weight, off)


def first_last_kernel(x_near, x_far, weight, before, out, cells, total):
    gx, nx = lax.axis_index("gx"), lax.axis_size("gx")
    odd_x = lax.rem(gx, 2)
    cells[1 - odd_x] = x_near[...]
    cells[odd_x] = jnp.where((gx > 0) & (gx < nx - 1), x_far[...].astype(F32), 0.0).astype(BF)
    rows = [[cells[k // 3, k % 3, plane] for plane in range(3)] for k in range(6)]
    total[...] = before[...]
    for off in range(3):
        part = rows_sum(rows[off : off + 4], weight, off)
        below = 3 - off
        total[0:below] += part[0:below]
        total[7 - off : 8] += part[below:]
    masked_rows(leaky_unit(total[...]), 2, out)


def deep_sum(planes, at, weight):
    left = jnp.concatenate([three_rows(p, 0, p.shape[0] - 2) for p in planes], axis=1)
    right = jnp.concatenate(
        [
            jnp.concatenate([weight[:, place, d].reshape(768, 256) for place in at], axis=0)
            for d in range(3)
        ],
        axis=1,
    )
    products = jnp.dot(left, right, preferred_element_type=F32)
    products = [products[:, d * 256 : d * 256 + 256] for d in range(3)]
    return depth_sum(*products, 32)


def second_own_kernel(own, y_near, weight, total):
    side, _ = sides()
    total[...] = deep_sum((own, y_near), (1, 2 * side), weight)


def second_far_kernel(y_far, weight, before, out):
    _, side = sides()
    gy, ny = lax.axis_index("gy"), lax.axis_size("gy")
    far = jnp.where((gy > 0) & (gy < ny - 1), deep_sum((y_far,), (2 * side,), weight), 0.0)
    masked_rows(leaky_unit(before[...] + far).reshape(6, 32, 256), 1, out)


def beside_own_kernel(own, y_far, weight, total):
    _, side = sides()
    total[...] = deep_sum((own, y_far), (2 - 2 * side, 1), weight)


def beside_far_kernel(beyond, weight, before, out):
    _, side = sides()
    values = before[...] + deep_sum((beyond,), (2 * side,), weight)
    masked_rows(leaky_unit(values).reshape(6, 32, 256), 1, out)


def half_weights(weight, half):
    return lambda off, col, d: weight[off, col, d, half * 128 : half * 128 + 128]


def lift(cells, up, b, upward, col):
    parts = jnp.concatenate([up[a, b, d] for a in range(2) for d in range(2)], axis=1)
    lifted = leaky_unit(jnp.dot(cells, parts, preferred_element_type=F32))
    for a in range(2):
        for d in range(2):
            lane = (2 * a + d) * 128
            part = lifted[:, lane : lane + 128].reshape(6, 32, 128)
            for i in range(6):
                row = 2 * i + a - 1
                if 0 <= row < 10:
                    upward[row, col, pl.ds(d, 32, stride=2), :] = part[i]


def decode_skip_kernel(encoded, y_near, y_far, weight, total, own, near, far):
    part = half_weights(weight, 1)
    put_own(own, encoded)
    put_total(total, own_sum(own, part))
    for cells, source, side in zip((near, far), (y_near, y_far), sides()):
        clear_ends(cells)
        cells[1:9] = source[...]
        total[side] += side_sum(cells, part, side)


def decode_own_kernel(own, x_near, x_far, up, weight, before, total, cells, upward):
    lift(own[...].reshape(192, 256), up, 0, upward, 0)
    lift(own[...].reshape(192, 256), up, 1, upward, 1)
    for b in range(2):
        cells[:, :, b * 128 : b * 128 + 128] = upward[:, b].astype(BF)
    values = own_sum(cells, half_weights(weight, 0))
    for b in range(2):
        total[b] = before[b] + values[:, b * 128 : b * 128 + 128].reshape(8, 64, 128)
    add_rows(total, x_near, x_far, half_weights(weight, 1))


def decode_far_kernel(y_far, up, weight, before, decoded, cells, upward, column, sem):
    _, side = sides()
    gy, ny = lax.axis_index("gy"), lax.axis_size("gy")
    lift(y_far[...].reshape(192, 256), up, 1 - side, upward, 0)
    cells[...] = jnp.where((gy > 0) & (gy < ny - 1), upward[:, 0], 0.0).astype(BF)
    values = before[side] + side_sum(cells, half_weights(weight, 0), side)
    column[...] = leaky_unit(values).astype(BF)
    copy = pltpu.make_async_copy(column, decoded.at[:, side], sem)
    copy.start()
    copy.wait()


def decode_near_kernel(y_near, up, weight, before, _, decoded, cells, upward, column, sems):
    side, _ = sides()
    lift(y_near[...].reshape(192, 256), up, 1 - side, upward, 0)
    cells[...] = upward[:, 0].astype(BF)
    copies = []
    for half in range(2):
        rows = slice(4 * half, 4 * half + 4)
        values = before[side, rows] + side_sum(cells, half_weights(weight, 0), side, 4 * half, 4)
        column[rows] = leaky_unit(values).astype(BF)
        copies.append(
            pltpu.make_async_copy(column.at[rows], decoded.at[rows, side], sems.at[half])
        )
        copies[-1].start()
    for copy in copies:
        copy.wait()


def call(kernel, outs, scratch, name, flops, *operands, remote=(), hbm_out=False, aliases=()):
    vmem = pl.BlockSpec(memory_space=pltpu.VMEM)
    hbm = pl.BlockSpec(memory_space=pltpu.HBM)
    return pl.pallas_call(
        kernel,
        out_shape=[jax.ShapeDtypeStruct(shape, dtype) for shape, dtype in outs],
        in_specs=[hbm if i in remote else vmem for i in range(len(operands))],
        out_specs=[hbm if hbm_out else vmem] * len(outs),
        scratch_shapes=[
            pltpu.SemaphoreType.DMA(shape) if dtype is None else pltpu.VMEM(shape, dtype)
            for shape, dtype in scratch
        ],
        compiler_params=pltpu.CompilerParams(vmem_limit_bytes=LIMIT),
        cost_estimate=pl.CostEstimate(flops=flops, bytes_accessed=1 << 20, transcendentals=0),
        input_output_aliases=dict(aliases),
        name=name,
    )(*operands)


def swap_near(cells):
    return lax.ppermute(cells, "gy", [(i, i ^ 1) for i in range(lax.axis_size("gy"))])


def swap_far(cells):
    nx, ny = lax.axis_size("gx"), lax.axis_size("gy")
    far = []
    for x in range(nx):
        for y in range(ny):
            to = (x ^ 1) * ny + y if y in (0, ny - 1) else x * ny + ((y + 1) ^ 1) - 1
            far.append((x * ny + y, to))
    far = far[ny // 2 - 1 :] + far[: ny // 2 - 1]
    return lax.ppermute(cells, ("gx", "gy"), far)


def swap_y(near_cells, far_cells):
    near, far = swap_near(near_cells), swap_far(far_cells)
    at, ny = lax.axis_index("gy"), lax.axis_size("gy")
    far = jnp.where((at > 0) & (at < ny - 1), far, jnp.zeros_like(far))
    return lax.optimization_barrier((near, far))


def swap_x(near_cells, far_cells):
    nx, ny = lax.axis_size("gx"), lax.axis_size("gy")
    near = [(i, i ^ 1) for i in range(nx)]
    far = []
    for x in range(nx):
        for y in range(ny):
            idle = y ^ 4 if ny >= 8 else y ^ 1
            to = x * ny + idle if x in (0, nx - 1) else (((x + 1) ^ 1) - 1) * ny + y
            far.append((x * ny + y, to))
    got = lax.ppermute(near_cells, "gx", near)
    return got, lax.ppermute(far_cells, ("gx", "gy"), far)


def local(
    volume,
    weight_entry,
    weight_down,
    weight_deep_first,
    weight_deep_second,
    weight_upward,
    weight_decoder,
):
    odd_x = lax.rem(lax.axis_index("gx"), 2)
    odd_y = lax.rem(lax.axis_index("gy"), 2)

    def column(array, at):
        return lax.dynamic_index_in_dim(array, at, axis=1, keepdims=False)

    def rows(array, at, count):
        return lax.dynamic_slice_in_dim(array, at, count, axis=0)

    def four_columns(pair, y_near, y_far, at):
        near, far = rows(y_near, at, 1), rows(y_far, at, 1)
        low = jnp.where(odd_y == 1, near, far)
        high = jnp.where(odd_y == 1, far, near)
        return jnp.concatenate([low, pair, high], axis=0)

    at_near, at_far = 7 * (1 - odd_x), 7 * odd_x
    sums = ((2, 8, 64, 128), F32)
    line = ((8, 64, 128), BF)
    tall = ((10, 64, 128), BF)
    wide = ((10, 64, 256), BF)
    own, near, far, edge_near, edge_far = call(
        prep_kernel,
        [((8, 2, 64, 128), BF), line, line, ((2, 64, 128), BF), ((2, 64, 128), BF)],
        [((), None)],
        "prep",
        1_000_000,
        volume,
        remote=(0,),
    )
    y1, y2 = swap_y(near, far)
    (total,) = call(
        entry_own_kernel, [sums], [wide], "entry_own", 600_000_000, own, weight_entry
    )
    x1, x2 = swap_x(
        four_columns(edge_near, y1, y2, at_near), four_columns(edge_far, y1, y2, at_far)
    )
    (total,) = call(
        entry_side_kernel,
        [sums],
        [tall, tall],
        "entry_side",
        1_000_000_000,
        y1,
        y2,
        weight_entry,
        total,
    )
    encoded, coarse = call(
        entry_last_kernel,
        [((8, 2, 64, 128), BF), ((4, 32, 256), BF)],
        [((8, 2, 64, 128), F32), sums],
        "entry_last",
        1_000_000_000,
        x1,
        x2,
        weight_entry,
        weight_down,
        total,
    )

    g1, g2 = swap_y(column(encoded, 1 - odd_y), column(encoded, odd_y))
    c1, c2 = swap_y(coarse, coarse)
    c_low = jnp.where(odd_y == 1, c1, c2)
    c_high = jnp.where(odd_y == 1, c2, c1)

    def coarse_edge(at):
        return jnp.stack([rows(c_low, at, 3), rows(coarse, at, 3), rows(c_high, at, 3)], axis=1)

    d1, d2 = swap_x(coarse_edge(1 - odd_x), coarse_edge(odd_x))
    (part,) = call(
        first_own_kernel,
        [((8, 32, 256), F32)],
        [((3, 4, 32, 256), BF)],
        "first_own",
        700_000_000,
        coarse,
        c1,
        c2,
        weight_deep_first,
    )
    (deep_one,) = call(
        first_last_kernel,
        [((8, 32, 256), BF)],
        [((2, 3, 3, 32, 256), BF), ((8, 32, 256), F32)],
        "first_last",
        1_000_000_000,
        d1,
        d2,
        weight_deep_first,
        part,
    )
    f1, f2 = swap_near(deep_one), swap_far(deep_one)
    f3 = swap_far(f1)
    skip, _ = lax.optimization_barrier(((encoded, g1, g2), deep_one))
    (total,) = call(
        decode_skip_kernel,
        [sums],
        [wide, tall, tall],
        "decode_skip",
        2_000_000_000,
        *skip,
        weight_decoder,
    )
    edges = (
        four_columns(rows(encoded, at_near, 1)[0], g1, g2, at_near),
        four_columns(rows(encoded, at_far, 1)[0], g1, g2, at_far),
    )
    edges, _ = lax.optimization_barrier((edges, deep_one))
    e1, e2 = swap_x(*edges)
    sum_two, two = ((192, 256), F32), ((6, 32, 256), BF)
    (part,) = call(
        second_own_kernel, [sum_two], [], "second_own", 1000, deep_one, f1, weight_deep_second
    )
    (deep_two,) = call(
        second_far_kernel, [two], [], "second_far", 1000, f2, weight_deep_second, part
    )
    h1 = swap_near(deep_two)
    (part,) = call(
        beside_own_kernel, [sum_two], [], "beside_own", 1000, deep_one, f2, weight_deep_second
    )
    (beside,) = call(
        beside_far_kernel, [two], [], "beside_far", 1000000000, f3, weight_deep_second, part
    )
    upward = ((10, 1, 64, 128), F32)
    (total,) = call(
        decode_own_kernel,
        [sums],
        [wide, ((10, 2, 64, 128), F32)],
        "decode_own",
        1000,
        deep_two,
        e1,
        e2,
        weight_upward,
        weight_decoder,
        total,
    )
    (decoded,) = call(
        decode_far_kernel,
        [((8, 2, 64, 128), BF)],
        [tall, upward, line, ((), None)],
        "decode_far",
        2000000000,
        beside,
        weight_upward,
        weight_decoder,
        total,
        hbm_out=True,
    )
    (decoded,) = call(
        decode_near_kernel,
        [((8, 2, 64, 128), BF)],
        [tall, upward, line, ((2,), None)],
        "decode_near",
        1000,
        h1,
        weight_upward,
        weight_decoder,
        total,
        decoded,
        remote=(4,),
        hbm_out=True,
        aliases=((4, 0),),
    )
    return decoded


def solution(mesh):
    return jax.shard_map(
        local,
        mesh=mesh,
        in_specs=(P("gx", "gy", None, None), P(), P(), P(), P(), P(), P()),
        out_specs=P("gx", "gy", None, None),
        check_vma=False,
    )
```

```python
import jax
import jax.numpy as jnp
from jax import lax
from jax.experimental import pallas as pl
from jax.experimental.pallas import tpu as pltpu
from jax.sharding import PartitionSpec as P

BF = jnp.bfloat16
F32 = jnp.float32
LIMIT = 20 * 1024 * 1024


def leaky_unit(values):
    return jnp.where(values > 0, values, 0.1 * values)


def depth_sum(before, here, after, depth):
    at = lax.rem(lax.broadcasted_iota(jnp.int32, here.shape, 0), depth)
    count = here.shape[0]
    before = jnp.where(at == 0, 0.0, pltpu.roll(before, 1, axis=0))
    after = jnp.where(at == depth - 1, 0.0, pltpu.roll(after, count - 1, axis=0))
    return before + here + after


def three_rows(cells, first, rows):
    lanes = cells.shape[2]
    return jnp.concatenate(
        [
            cells[first + off : first + off + rows].reshape(rows * cells.shape[1], lanes)
            for off in range(3)
        ],
        axis=1,
    )


def own_sum(cells, part):
    left = three_rows(cells, 0, 8)
    products = []
    for d in range(3):
        blocks = []
        for off in range(3):
            blocks.append(jnp.concatenate([part(off, 1, d), part(off, 0, d)], axis=1))
            blocks.append(jnp.concatenate([part(off, 2, d), part(off, 1, d)], axis=1))
        products.append(
            jnp.dot(left, jnp.concatenate(blocks, axis=0), preferred_element_type=F32)
        )
    return depth_sum(*products, 64)


def taps_sum(left, blocks):
    right = jnp.concatenate([jnp.concatenate(parts, axis=0) for parts in blocks], axis=1)
    products = jnp.dot(left, right, preferred_element_type=F32)
    return depth_sum(*[products[:, d * 128 : d * 128 + 128] for d in range(3)], 64)


def side_sum(cells, part, side, first=0, rows=8):
    blocks = [[part(off, 2 * side, d) for off in range(3)] for d in range(3)]
    return taps_sum(three_rows(cells, first, rows), blocks).reshape(rows, 64, 128)


def add_rows(total, x_near, x_far, part):
    gx, nx = lax.axis_index("gx"), lax.axis_size("gx")
    odd_x = lax.rem(gx, 2)
    for cells, high, ok in ((x_near, 1 - odd_x, None), (x_far, odd_x, (gx > 0) & (gx < nx - 1))):
        left = jnp.concatenate(
            [jnp.concatenate([cells[b + col] for col in range(3)], axis=1) for b in range(2)],
            axis=0,
        )
        blocks = [[part(2 * high, col, d) for col in range(3)] for d in range(3)]
        values = taps_sum(left, blocks)
        if ok is not None:
            values = jnp.where(ok, values, 0.0)
        for b in range(2):
            total[b, 7 * high] += values[b * 64 : b * 64 + 64]


def sides():
    odd = lax.rem(lax.axis_index("gy"), 2)
    return 1 - odd, odd


def clear_ends(cells):
    cells[0] = jnp.zeros_like(cells[0])
    cells[9] = jnp.zeros_like(cells[9])


def put_own(cells, own):
    clear_ends(cells)
    for b in range(2):
        cells[1:9, :, b * 128 : b * 128 + 128] = own[:, b]


def put_total(total, values):
    for b in range(2):
        total[b] = values[:, b * 128 : b * 128 + 128].reshape(8, 64, 128)


def prep_kernel(volume, own, near, far, edge_near, edge_far, sem):
    copy = pltpu.make_async_copy(volume, own, sem)
    copy.start()
    odd_x, odd_y = lax.rem(lax.axis_index("gx"), 2), lax.rem(lax.axis_index("gy"), 2)
    copy.wait()
    near[...] = own[:, 1 - odd_y]
    far[...] = own[:, odd_y]
    edge_near[...] = own[7 * (1 - odd_x)]
    edge_far[...] = own[7 * odd_x]


def entry_own_kernel(own, weight, total, cells):
    put_own(cells, own)
    put_total(total, own_sum(cells, lambda off, col, d: weight[off, col, d]))


def entry_side_kernel(y_near, y_far, weight, before, total, near, far):
    part = lambda off, col, d: weight[off, col, d]
    for cells, source, side in zip((near, far), (y_near, y_far), sides()):
        clear_ends(cells)
        cells[1:9] = source[...]
        total[side] = before[side] + side_sum(cells, part, side)


def entry_last_kernel(x_near, x_far, weight, down, before, encoded, coarse, fine, total):
    total[:, 0] = before[:, 0]
    total[:, 7] = before[:, 7]
    add_rows(total, x_near, x_far, lambda off, col, d: weight[off, col, d])

    def finish(row, source):
        for b in range(2):
            half = leaky_unit(source[b, row]).astype(BF)
            encoded[row, b] = half
            fine[row, b] = half.astype(F32)

    for row in range(1, 7):
        finish(row, before)
    finish(0, total)
    finish(7, total)
    small = jnp.zeros((128, 256), F32)
    for a in range(2):
        for d in range(2):
            cells = jnp.concatenate(
                [
                    jnp.concatenate(
                        [fine[2 * i + a, b, pl.ds(d, 32, stride=2), :] for b in range(2)], axis=1
                    )
                    for i in range(4)
                ],
                axis=0,
            ).astype(BF)
            small = small + jnp.dot(
                cells, down[a, :, d].reshape(256, 256), preferred_element_type=F32
            )
    coarse[...] = leaky_unit(small).astype(BF).reshape(4, 32, 256)


def masked_rows(result, beyond, out):
    rows = out.shape[0]
    gx, nx = lax.axis_index("gx"), lax.axis_size("gx")
    out[0:beyond] = jnp.where(gx > 0, result[0:beyond], 0.0).astype(BF)
    out[beyond : rows - beyond] = result[beyond : rows - beyond].astype(BF)
    out[rows - beyond :] = jnp.where(gx < nx - 1, result[rows - beyond :], 0.0).astype(BF)


def rows_sum(rows, weight, off):
    left = jnp.concatenate([jnp.concatenate(planes, axis=1) for planes in rows], axis=0)
    right = jnp.concatenate([weight[off, :, d].reshape(768, 256) for d in range(3)], axis=1)
    products = jnp.dot(left, right, preferred_element_type=F32)
    products = [products[:, d * 256 : d * 256 + 256] for d in range(3)]
    return depth_sum(*products, 32).reshape(len(rows), 32, 256)


def first_own_kernel(own, y_near, y_far, weight, total, cells):
    near, far = sides()
    cells[1] = own[...]
    cells[2 * near] = y_near[...]
    cells[2 * far] = y_far[...]
    rows = [[cells[plane, row] for plane in range(3)] for row in range(4)]
    total[...] = jnp.zeros_like(total)
    for off in range(3):
        total[3 - off : 7 - off] += rows_sum(rows, weight, off)


def first_last_kernel(x_near, x_far, weight, before, out, cells, total):
    gx, nx = lax.axis_index("gx"), lax.axis_size("gx")
    odd_x = lax.rem(gx, 2)
    cells[1 - odd_x] = x_near[...]
    cells[odd_x] = jnp.where((gx > 0) & (gx < nx - 1), x_far[...].astype(F32), 0.0).astype(BF)
    rows = [[cells[k // 3, k % 3, plane] for plane in range(3)] for k in range(6)]
    total[...] = before[...]
    for off in range(3):
        part = rows_sum(rows[off : off + 4], weight, off)
        below = 3 - off
        total[0:below] += part[0:below]
        total[7 - off : 8] += part[below:]
    masked_rows(leaky_unit(total[...]), 2, out)


def deep_sum(planes, at, weight):
    left = jnp.concatenate([three_rows(p, 0, p.shape[0] - 2) for p in planes], axis=1)
    right = jnp.concatenate(
        [
            jnp.concatenate([weight[:, place, d].reshape(768, 256) for place in at], axis=0)
            for d in range(3)
        ],
        axis=1,
    )
    products = jnp.dot(left, right, preferred_element_type=F32)
    products = [products[:, d * 256 : d * 256 + 256] for d in range(3)]
    return depth_sum(*products, 32)


def second_own_kernel(own, y_near, weight, total):
    side, _ = sides()
    total[...] = deep_sum((own, y_near), (1, 2 * side), weight)


def second_far_kernel(y_far, weight, before, out):
    _, side = sides()
    gy, ny = lax.axis_index("gy"), lax.axis_size("gy")
    far = jnp.where((gy > 0) & (gy < ny - 1), deep_sum((y_far,), (2 * side,), weight), 0.0)
    masked_rows(leaky_unit(before[...] + far).reshape(6, 32, 256), 1, out)


def beside_own_kernel(own, y_far, weight, total):
    _, side = sides()
    total[...] = deep_sum((own, y_far), (2 - 2 * side, 1), weight)


def beside_far_kernel(beyond, weight, before, out):
    _, side = sides()
    values = before[...] + deep_sum((beyond,), (2 * side,), weight)
    masked_rows(leaky_unit(values).reshape(6, 32, 256), 1, out)


def half_weights(weight, half):
    return lambda off, col, d: weight[off, col, d, half * 128 : half * 128 + 128]


def lift(cells, up, b, upward, col):
    parts = jnp.concatenate([up[a, b, d] for a in range(2) for d in range(2)], axis=1)
    lifted = leaky_unit(jnp.dot(cells, parts, preferred_element_type=F32))
    for a in range(2):
        for d in range(2):
            lane = (2 * a + d) * 128
            part = lifted[:, lane : lane + 128].reshape(6, 32, 128)
            for i in range(6):
                row = 2 * i + a - 1
                if 0 <= row < 10:
                    upward[row, col, pl.ds(d, 32, stride=2), :] = part[i]


def decode_skip_kernel(encoded, y_near, y_far, weight, total, own, near, far):
    part = half_weights(weight, 1)
    put_own(own, encoded)
    put_total(total, own_sum(own, part))
    for cells, source, side in zip((near, far), (y_near, y_far), sides()):
        clear_ends(cells)
        cells[1:9] = source[...]
        total[side] += side_sum(cells, part, side)


def decode_own_kernel(own, x_near, x_far, up, weight, before, total, cells, upward):
    lift(own[...].reshape(192, 256), up, 0, upward, 0)
    lift(own[...].reshape(192, 256), up, 1, upward, 1)
    for b in range(2):
        cells[:, :, b * 128 : b * 128 + 128] = upward[:, b].astype(BF)
    values = own_sum(cells, half_weights(weight, 0))
    for b in range(2):
        total[b] = before[b] + values[:, b * 128 : b * 128 + 128].reshape(8, 64, 128)
    add_rows(total, x_near, x_far, half_weights(weight, 1))


def decode_far_kernel(y_far, up, weight, before, column, cells, upward):
    _, side = sides()
    gy, ny = lax.axis_index("gy"), lax.axis_size("gy")
    lift(y_far[...].reshape(192, 256), up, 1 - side, upward, 0)
    cells[...] = jnp.where((gy > 0) & (gy < ny - 1), upward[:, 0], 0.0).astype(BF)
    values = before[side] + side_sum(cells, half_weights(weight, 0), side)
    column[...] = leaky_unit(values).astype(BF)


def decode_near_kernel(
    y_near, up, weight, before, far_column, decoded, cells, upward, column, sems
):
    side, side_far = sides()
    copies = [pltpu.make_async_copy(far_column, decoded.at[:, side_far], sems.at[2])]
    copies[0].start()
    lift(y_near[...].reshape(192, 256), up, 1 - side, upward, 0)
    cells[...] = upward[:, 0].astype(BF)
    for half in range(2):
        rows = slice(4 * half, 4 * half + 4)
        values = before[side, rows] + side_sum(cells, half_weights(weight, 0), side, 4 * half, 4)
        column[rows] = leaky_unit(values).astype(BF)
        copies.append(
            pltpu.make_async_copy(column.at[rows], decoded.at[rows, side], sems.at[half])
        )
        copies[-1].start()
    for copy in copies:
        copy.wait()


def call(kernel, outs, scratch, name, flops, *operands, remote=(), hbm_out=False, aliases=()):
    vmem = pl.BlockSpec(memory_space=pltpu.VMEM)
    hbm = pl.BlockSpec(memory_space=pltpu.HBM)
    return pl.pallas_call(
        kernel,
        out_shape=[jax.ShapeDtypeStruct(shape, dtype) for shape, dtype in outs],
        in_specs=[hbm if i in remote else vmem for i in range(len(operands))],
        out_specs=[hbm if hbm_out else vmem] * len(outs),
        scratch_shapes=[
            pltpu.SemaphoreType.DMA(shape) if dtype is None else pltpu.VMEM(shape, dtype)
            for shape, dtype in scratch
        ],
        compiler_params=pltpu.CompilerParams(vmem_limit_bytes=LIMIT),
        cost_estimate=pl.CostEstimate(flops=flops, bytes_accessed=1 << 20, transcendentals=0),
        input_output_aliases=dict(aliases),
        name=name,
    )(*operands)


def swap_near(cells):
    return lax.ppermute(cells, "gy", [(i, i ^ 1) for i in range(lax.axis_size("gy"))])


def swap_far(cells):
    nx, ny = lax.axis_size("gx"), lax.axis_size("gy")
    far = []
    for x in range(nx):
        for y in range(ny):
            to = (x ^ 1) * ny + y if y in (0, ny - 1) else x * ny + ((y + 1) ^ 1) - 1
            far.append((x * ny + y, to))
    far = far[ny // 2 - 1 :] + far[: ny // 2 - 1]
    return lax.ppermute(cells, ("gx", "gy"), far)


def swap_y(near_cells, far_cells):
    near, far = swap_near(near_cells), swap_far(far_cells)
    at, ny = lax.axis_index("gy"), lax.axis_size("gy")
    far = jnp.where((at > 0) & (at < ny - 1), far, jnp.zeros_like(far))
    return lax.optimization_barrier((near, far))


def swap_x(near_cells, far_cells):
    nx, ny = lax.axis_size("gx"), lax.axis_size("gy")
    near = [(i, i ^ 1) for i in range(nx)]
    far = []
    for x in range(nx):
        for y in range(ny):
            idle = y ^ 4 if ny >= 8 else y ^ 1
            to = x * ny + idle if x in (0, nx - 1) else (((x + 1) ^ 1) - 1) * ny + y
            far.append((x * ny + y, to))
    got = lax.ppermute(near_cells, "gx", near)
    return got, lax.ppermute(far_cells, ("gx", "gy"), far)


def local(
    volume,
    weight_entry,
    weight_down,
    weight_deep_first,
    weight_deep_second,
    weight_upward,
    weight_decoder,
):
    odd_x = lax.rem(lax.axis_index("gx"), 2)
    odd_y = lax.rem(lax.axis_index("gy"), 2)

    def column(array, at):
        return lax.dynamic_index_in_dim(array, at, axis=1, keepdims=False)

    def rows(array, at, count):
        return lax.dynamic_slice_in_dim(array, at, count, axis=0)

    def four_columns(pair, y_near, y_far, at):
        near, far = rows(y_near, at, 1), rows(y_far, at, 1)
        low = jnp.where(odd_y == 1, near, far)
        high = jnp.where(odd_y == 1, far, near)
        return jnp.concatenate([low, pair, high], axis=0)

    at_near, at_far = 7 * (1 - odd_x), 7 * odd_x
    sums = ((2, 8, 64, 128), F32)
    line = ((8, 64, 128), BF)
    tall = ((10, 64, 128), BF)
    wide = ((10, 64, 256), BF)
    own, near, far, edge_near, edge_far = call(
        prep_kernel,
        [((8, 2, 64, 128), BF), line, line, ((2, 64, 128), BF), ((2, 64, 128), BF)],
        [((), None)],
        "prep",
        1_000_000,
        volume,
        remote=(0,),
    )
    y1, y2 = swap_y(near, far)
    (total,) = call(
        entry_own_kernel, [sums], [wide], "entry_own", 600_000_000, own, weight_entry
    )
    x1, x2 = swap_x(
        four_columns(edge_near, y1, y2, at_near), four_columns(edge_far, y1, y2, at_far)
    )
    (total,) = call(
        entry_side_kernel,
        [sums],
        [tall, tall],
        "entry_side",
        1_000_000_000,
        y1,
        y2,
        weight_entry,
        total,
    )
    encoded, coarse = call(
        entry_last_kernel,
        [((8, 2, 64, 128), BF), ((4, 32, 256), BF)],
        [((8, 2, 64, 128), F32), sums],
        "entry_last",
        1_000_000_000,
        x1,
        x2,
        weight_entry,
        weight_down,
        total,
    )

    g1, g2 = swap_y(column(encoded, 1 - odd_y), column(encoded, odd_y))
    c1, c2 = swap_y(coarse, coarse)
    c_low = jnp.where(odd_y == 1, c1, c2)
    c_high = jnp.where(odd_y == 1, c2, c1)

    def coarse_edge(at):
        return jnp.stack([rows(c_low, at, 3), rows(coarse, at, 3), rows(c_high, at, 3)], axis=1)

    d1, d2 = swap_x(coarse_edge(1 - odd_x), coarse_edge(odd_x))
    (part,) = call(
        first_own_kernel,
        [((8, 32, 256), F32)],
        [((3, 4, 32, 256), BF)],
        "first_own",
        700_000_000,
        coarse,
        c1,
        c2,
        weight_deep_first,
    )
    (deep_one,) = call(
        first_last_kernel,
        [((8, 32, 256), BF)],
        [((2, 3, 3, 32, 256), BF), ((8, 32, 256), F32)],
        "first_last",
        1_000_000_000,
        d1,
        d2,
        weight_deep_first,
        part,
    )
    f1, f2 = swap_near(deep_one), swap_far(deep_one)
    f3 = swap_far(f1)
    skip, _ = lax.optimization_barrier(((encoded, g1, g2), deep_one))
    (total,) = call(
        decode_skip_kernel,
        [sums],
        [wide, tall, tall],
        "decode_skip",
        2_000_000_000,
        *skip,
        weight_decoder,
    )
    edges = (
        four_columns(rows(encoded, at_near, 1)[0], g1, g2, at_near),
        four_columns(rows(encoded, at_far, 1)[0], g1, g2, at_far),
    )
    edges, _ = lax.optimization_barrier((edges, deep_one))
    e1, e2 = swap_x(*edges)
    sum_two, two = ((192, 256), F32), ((6, 32, 256), BF)
    (part,) = call(
        second_own_kernel, [sum_two], [], "second_own", 1000, deep_one, f1, weight_deep_second
    )
    (deep_two,) = call(
        second_far_kernel, [two], [], "second_far", 1000, f2, weight_deep_second, part
    )
    h1 = swap_near(deep_two)
    (part,) = call(
        beside_own_kernel, [sum_two], [], "beside_own", 1000, deep_one, f2, weight_deep_second
    )
    (beside,) = call(
        beside_far_kernel, [two], [], "beside_far", 1000000000, f3, weight_deep_second, part
    )
    upward = ((10, 1, 64, 128), F32)
    (total,) = call(
        decode_own_kernel,
        [sums],
        [wide, ((10, 2, 64, 128), F32)],
        "decode_own",
        1000,
        deep_two,
        e1,
        e2,
        weight_upward,
        weight_decoder,
        total,
    )
    (far_column,) = call(
        decode_far_kernel,
        [line],
        [tall, upward],
        "decode_far",
        2000000000,
        beside,
        weight_upward,
        weight_decoder,
        total,
    )
    (decoded,) = call(
        decode_near_kernel,
        [((8, 2, 64, 128), BF)],
        [tall, upward, line, ((3,), None)],
        "decode_near",
        1000,
        h1,
        weight_upward,
        weight_decoder,
        total,
        far_column,
        hbm_out=True,
    )
    return decoded


def solution(mesh):
    return jax.shard_map(
        local,
        mesh=mesh,
        in_specs=(P("gx", "gy", None, None), P(), P(), P(), P(), P(), P()),
        out_specs=P("gx", "gy", None, None),
        check_vma=False,
    )
```
